768 devices in a mesh: db: 64 (over y, x, core), mp: 12 (over z).
Axes of the slice: x: 4, y: 8, z: 12, core: 2. Of those that a mesh axis runs over, the one named last changes fastest.
Arguments:
- hidden: bfloat16 [49152, 4096], P(('db', 'mp')), may hold values from -6 to 6
- norm_gain: float32 [4096], replicated, may hold values from 0.25 to 1.75
- query_weight: bfloat16 [4096, 3072], P(None, 'mp'), may hold values from -0.09375 to 0.09375
- key_weight: bfloat16 [4096, 3072], P(None, 'mp'), may hold values from -0.09375 to 0.09375
- value_weight: bfloat16 [4096, 3072], P(None, 'mp'), may hold values from -0.09375 to 0.09375
- bank: bfloat16 [256, 128, 4096], P('db'), may hold values from -6 to 6
- neighbour_ids: int32 [768, 2], P('db'), may hold values from 0 to 255, as said below
Outputs:
- attended: bfloat16 [49152, 3072], P('db', 'mp')
The draws below stay inside these ranges and needn't reach their ends.
Inputs may be any that keep to these rules, and one draw needn't show every extreme that they name: `neighbour_ids`: the 12 rows of one db index name at most 1 ids in the range of any one shard (ids j*4 to (j+1)*4 - 1), and exactly 1 in some shard.
All inputs are finite; a program needn't handle non-finite values.
Results may differ from the reference program's by a relative error of at most 0.025.
Values may be sent and summed in bfloat16 or wider, within the bound.
A program may use at most 64 MiB of HBM per device.

```python
import jax
import jax.numpy as jnp
from jax import lax

D = 4096
HD = 128
BLOCK = 64
NBR_LEN = 128
K = 2
BANK_DEV = 4
HEADS = 24
BLOCKS_DEV = 12
CAP = 1
TOKENS = 49152
BLOCKS = 768
BANK = 256


def draw_neighbour_ids(key, part):
    key = jax.random.fold_in(key, 11)
    shards = BLOCKS // BLOCKS_DEV
    wanted = BLOCKS_DEV * K
    chosen_count = (wanted + CAP - 1) // CAP
    popular = jax.random.randint(jax.random.fold_in(key, 1), (shards,), 0, 1 << 21)

    def one_device(device_key):
        noise = jax.random.randint(device_key, (shards,), 0, 1 << 20)
        score = (popular + noise) * shards + jnp.arange(shards, dtype=jnp.int32)
        _, chosen = lax.top_k(score, chosen_count)
        owner_list = chosen[jnp.arange(wanted, dtype=jnp.int32) // CAP]
        shuffled = jax.random.permutation(jax.random.fold_in(device_key, 1), owner_list)
        rows_in = jax.random.randint(jax.random.fold_in(device_key, 2), (wanted,), 0, BANK_DEV)
        return (shuffled * BANK_DEV + rows_in).astype(jnp.int32)
    device_keys = jax.random.split(jax.random.fold_in(key, 2), shards)
    return jax.vmap(one_device)(device_keys).reshape(BLOCKS, K)


def steps_of(own_key, shape, cuts, smallest, top_value):
    loudness = 1.0
    for axis_at, shards_of in cuts:
        heights = jax.random.uniform(jax.random.fold_in(jax.random.fold_in(own_key, 6), axis_at), (shards_of,), jnp.float32, smallest / len(cuts), top_value / len(cuts))
        loudness = loudness * jnp.repeat(jnp.exp(heights), shape[axis_at] // shards_of).reshape((-1,) + (1,) * (len(shape) - 1 - axis_at))
    return loudness


def gaussian(stream_key, extent, deviation, bound, cuts=(), kind=jnp.bfloat16):
    entries = jax.random.normal(stream_key, extent, jnp.float32) * deviation
    if len(cuts) > 0:
        entries = steps_of(stream_key, extent, cuts, -0.22, 0.18) * entries
    return jnp.clip(entries, min=-bound, max=bound).astype(kind)


def setup_inputs(seed: int = 0) -> dict:
    arg_keys = jax.random.split(jax.random.key(seed), 8)
    return {
        "hidden": gaussian(arg_keys[0], (TOKENS, D), 1.0, 6.0, ((0, 768),)),
        "norm_gain": jnp.clip(1.0 + 0.15 * jax.random.normal(arg_keys[1], (D,), jnp.float32), 0.25, 1.75),
        "query_weight": gaussian(arg_keys[2], (D, HEADS * HD), D ** -0.5, 0.09375, ((1, 12),)),
        "key_weight": gaussian(arg_keys[3], (D, HEADS * HD), D ** -0.5, 0.09375, ((1, 12),)),
        "value_weight": gaussian(arg_keys[4], (D, HEADS * HD), D ** -0.5, 0.09375, ((1, 12),)),
        "bank": gaussian(arg_keys[5], (BANK, NBR_LEN, D), 1.0, 6.0, ((0, 64),)),
        "neighbour_ids": draw_neighbour_ids(jax.random.fold_in(arg_keys[7], 71), 0),
    }


def reference(hidden, norm_gain, query_weight, key_weight, value_weight, bank, neighbour_ids):
    stream = hidden.astype(jnp.float32)
    normed = (stream * lax.rsqrt(lax.optimization_barrier(jnp.mean(stream * stream, axis=-1, keepdims=True)) + 1e-06) * norm_gain).astype(jnp.bfloat16)
    queries = (jnp.dot(normed, query_weight, preferred_element_type=jnp.float32) * HD ** (-0.5)).astype(jnp.bfloat16)
    flat_bank = bank.reshape(BANK * NBR_LEN, D)
    bank_keys = jnp.dot(flat_bank, key_weight, preferred_element_type=jnp.float32).astype(jnp.bfloat16).reshape(BANK, NBR_LEN, HEADS, HD)
    bank_values = jnp.dot(flat_bank, value_weight, preferred_element_type=jnp.float32).astype(jnp.bfloat16).reshape(BANK, NBR_LEN, HEADS, HD)
    query_blocks = queries.reshape(BLOCKS, BLOCK, HEADS, HD)

    def attend(inputs):
        block_queries, block_ids = inputs
        near_keys = jnp.take(bank_keys, block_ids, axis=0).astype(jnp.float32)
        near_values = jnp.take(bank_values, block_ids, axis=0).astype(jnp.float32)
        scores = jnp.einsum('qhd,nkhd->nhqk', block_queries.astype(jnp.float32), near_keys)
        expo = jnp.exp(scores)
        denom = lax.optimization_barrier(jnp.sum(expo, axis=-1, keepdims=True))
        lse = jnp.log(denom)[..., 0]
        probs = (expo / denom).astype(jnp.bfloat16)
        part = jnp.einsum('nhqk,nkhd->nqhd', probs.astype(jnp.float32), near_values).astype(jnp.bfloat16)
        lse_tq = jnp.transpose(lse, (0, 2, 1))
        total = jnp.log(lax.optimization_barrier(jnp.sum(jnp.exp(lse_tq), axis=0, keepdims=True)))
        weights = jnp.exp(lse_tq - total)[..., None]
        return lax.optimization_barrier(jnp.sum(weights * part.astype(jnp.float32), axis=0)).astype(jnp.bfloat16)
    attended = lax.map(attend, (query_blocks, neighbour_ids)).reshape(TOKENS, HEADS * HD)
    return attended
```

```python
import jax
import jax.numpy as jnp
from jax import lax
from jax.experimental import pallas as pl
from jax.experimental.pallas import tpu as pltpu
from jax.sharding import PartitionSpec as P

HD = 128
BLOCK = 64
NBR = 128
EPS = 1e-6
NX, NY, NZ = 4, 8, 12
D = 4096
ROWS = 4
NEG = -1e30
RR = 80
MESH = pl.DeviceIdType.MESH
BF = jnp.bfloat16
F32 = jnp.float32


def kernel(
    hidden, gain, wq, wk, wv, bank, ids, out,
    hid_v, wq_v, wk_v, wv_v, bank_v, zb, kv, kvs, qs, q_in, r_out, r_in, ids_v, ids_s,
    lsem, z_ss, z_rs, y_ss, y_rs, x_ss, x_rs, b_ss, b_rs, q_ss, q_rs, r_ss, r_rs, i_ss, i_rs,
):
    db = lax.axis_index("db")
    z = lax.axis_index("mp")
    c = db % 2
    x = (db // 2) % NX
    y = db // (2 * NX)
    x0 = x % 2
    x1 = x // 2

    def dev(yy, xx, cc, zz):
        return {"db": (yy * NX + xx) * 2 + cc, "mp": zz}

    xs = (x, x + 1 - 2 * x0, (x + 2) % NX, NX - 1 - x)
    z_dev = (dev(y, x, c, (z + 1) % NZ), dev(y, x, c, (z + NZ - 1) % NZ))
    y_dev = (dev((y + 1) % NY, x, c, z), dev((y + NY - 1) % NY, x, c, z))
    x_dev = tuple(dev(y, xx, c, z) for xx in xs)
    sib = dev(y, x, 1 - c, z)
    peers = z_dev + y_dev + x_dev[1:] + (sib,)

    loads = [
        pltpu.make_async_copy(a, b, lsem.at[n])
        for n, (a, b) in enumerate(
            ((hidden, hid_v), (bank, bank_v), (wk, wk_v), (wv, wv_v), (wq, wq_v), (ids, ids_v.at[0]))
        )
    ]
    for load in loads:
        load.start()
    barrier = pltpu.get_barrier_semaphore()
    for peer in peers:
        pl.semaphore_signal(barrier, inc=1, device_id=peer, device_id_type=MESH)

    def copy(src, dst, ss, rs, to):
        return pltpu.make_async_remote_copy(
            src_ref=src, dst_ref=dst, send_sem=ss, recv_sem=rs, device_id=to, device_id_type=MESH
        )

    sent = []

    def send(src, dst, ss, rs, to):
        one = copy(src, dst, ss, rs, to)
        one.start()
        sent.append(one)

    def landed(dst, ss, rs):
        copy(dst, dst, ss, rs, sib).wait_recv()

    loads[0].wait()

    def norm_rows(n, carry):
        rows = pl.ds(pl.multiple_of(n * 16, 16), 16)
        stream = hid_v[rows, :].astype(F32)
        factor = lax.rsqrt(jnp.mean(stream * stream, axis=-1, keepdims=True) + EPS)
        zb[0, rows, :] = (stream * factor * gain[...]).astype(BF)
        return carry

    lax.fori_loop(0, BLOCK // 16, norm_rows, 0)
    pl.semaphore_wait(barrier, len(peers))

    def z_part(slot, sub):
        return zb.at[slot, pl.ds(sub * 32, 32), :]

    def z_slot(way, s):
        return 0 if s == 0 else (11 if s == 6 else 2 * s - 1 + way)

    def z_send(way, s, sub):
        send(
            z_part(z_slot(way, s), sub), z_part(z_slot(way, s + 1), sub),
            z_ss.at[way, s, sub], z_rs.at[way, s, sub], z_dev[way],
        )

    def z_wait(way, s, sub):
        landed(z_part(z_slot(way, s), sub), z_ss.at[way, s - 1, sub], z_rs.at[way, s - 1, sub])

    def z_needed(way, s, sub):
        return s < 6 or sub == way

    for sub in range(2):
        for way in range(2):
            z_send(way, 0, sub)

    loads[5].wait()
    for j in (1, 2, 3):
        send(ids_v.at[0], ids_v.at[j], i_ss.at[j], i_rs.at[j], x_dev[j])

    def unit(yy, cc, bit):
        return ((yy * 2 + cc) * 2 + bit) * ROWS

    own = unit(y, c, x0)
    loads[1].wait()
    for which in range(2):
        loads[2 + which].wait()
        weight = (wk_v, wv_v)[which]

        def project(n, carry):
            got = jnp.dot(
                bank_v[pl.ds(n * 2, 2)].reshape(2 * NBR, D), weight[...], preferred_element_type=F32
            )
            low, high = got[:, :HD], got[:, HD:]
            mine = jnp.where(x0 == 0, low, high).astype(BF)
            other = jnp.where(x0 == 0, high, low).astype(BF)
            for a in range(2):
                kv[own + n * 2 + a, which] = mine[a * NBR : (a + 1) * NBR]
                kvs[n * 2 + a, which] = other[a * NBR : (a + 1) * NBR]
            return carry

        lax.fori_loop(0, ROWS // 2, project, 0)

    def y_at(way, s):
        return (y + NY - s) % NY if way == 0 else (y + s) % NY

    def kv_part(yy, cc, sub):
        return kv.at[pl.ds(unit(yy, cc, x0 if sub == 0 else 1 - x0), ROWS)]

    def y_send(way, s, sub):
        part = kv_part(y_at(way, s), c, sub)
        send(part, part, y_ss.at[way, s, sub], y_rs.at[way, s, sub], y_dev[way])

    def y_wait(way, s, sub):
        part = kv_part(y_at(way, s), c, sub)
        landed(part, y_ss.at[way, s - 1, sub], y_rs.at[way, s - 1, sub])

    def b_slot(way, s):
        return 0 if s == 0 else (7 if s == 4 else 2 * s - 1 + way)

    def b_send(way, s, sub):
        part = kv_part(y_at(way, s), c, sub)
        n = b_slot(way, s)
        send(part, part, b_ss.at[n, sub], b_rs.at[n, sub], sib)

    def b_wait(way, s, sub):
        n = b_slot(way, s)
        landed(kv_part(y_at(way, s), 1 - c, sub), b_ss.at[n, sub], b_rs.at[n, sub])

    send(kvs, kv.at[pl.ds(own, ROWS)], x_ss.at[0], x_rs.at[0], x_dev[1])
    for way in range(2):
        y_send(way, 0, 0)
    b_send(0, 0, 0)

    def y_needed(way, s, sub):
        return s < 4 or sub == way

    def y_step(s, sub):
        if s == 0:
            if sub == 1:
                landed(kv_part(y, c, 1), x_ss.at[0], x_rs.at[0])
                for way in range(2):
                    y_send(way, 0, 1)
                b_send(0, 0, 1)
            return
        for way in range(2):
            if y_needed(way, s, sub):
                y_wait(way, s, sub)
                if s < 4 and y_needed(way, s + 1, sub):
                    y_send(way, s, sub)
                b_send(way, s, sub)

    scale = HD ** (-0.5)

    def slots(g):
        return (0, 1) if g == 0 else ((11, 1) if g == 6 else (2 * g - 1, 2))

    def q_part(ref, g):
        first, count = slots(g)
        return ref.at[pl.ds(first, count)]

    def queries(g):
        first, count = slots(g)
        got = jnp.dot(
            zb[first : first + count].reshape(count * BLOCK, D), wq_v[...],
            preferred_element_type=F32,
        ) * scale
        low, high = got[:, :HD], got[:, HD:]
        mine = jnp.where(x0 == 0, low, high).astype(BF)
        other = jnp.where(x0 == 0, high, low).astype(BF)
        for a in range(count):
            q_in[0, first + a] = mine[a * BLOCK : (a + 1) * BLOCK]
            qs[first + a] = other[a * BLOCK : (a + 1) * BLOCK]
        for j in (2, 1, 3):
            src = q_part(q_in.at[0], g) if j == 2 else q_part(qs, g)
            send(src, q_part(q_in.at[j], g), q_ss.at[j, g], q_rs.at[j, g], x_dev[j])

    def block_of(slot):
        s = (slot + 1) // 2
        sign = 1 - 2 * (slot % 2)
        return (z + NZ + sign * s) % NZ

    diag = lax.broadcasted_iota(jnp.int32, (BLOCK, HD), 0) == lax.broadcasted_iota(
        jnp.int32, (BLOCK, HD), 1
    )
    row_no = lax.broadcasted_iota(jnp.int32, (16, HD), 0)

    def attend(j, slot):
        block = block_of(slot)
        q = q_in[j, slot]
        scores, rows = [], []
        for k in range(2):
            nbr = ids_s[j, block, k]
            shard = nbr // ROWS
            col = (shard // 2) % NX
            row = ((shard // (2 * NX) * 2 + shard % 2) * 2 + col % 2) * ROWS + nbr % ROWS
            s = lax.dot_general(q, kv[row, 0], (((1,), (1,)), ((), ())), preferred_element_type=F32)
            scores.append(jnp.where(col // 2 == x1, s, NEG))
            rows.append(row)
        top = jnp.max(jnp.maximum(scores[0], scores[1]), axis=-1, keepdims=True)
        e0 = jnp.exp(scores[0] - top)
        e1 = jnp.exp(scores[1] - top)
        denom = jnp.sum(e0 + e1, axis=-1, keepdims=True)
        o = jnp.dot(e0.astype(BF), kv[rows[0], 1], preferred_element_type=F32) + jnp.dot(
            e1.astype(BF), kv[rows[1], 1], preferred_element_type=F32
        )
        r_out[j, slot, 0:BLOCK, :] = (o / denom).astype(BF)
        lse = jnp.sum(jnp.where(diag, top + jnp.log(denom), 0.0), axis=0, keepdims=True)
        hi = lse.astype(BF).astype(F32)
        mid = (lse - hi).astype(BF).astype(F32)
        lo = lse - hi - mid
        packed = jnp.where(row_no == 0, hi, jnp.where(row_no == 1, mid, jnp.where(row_no == 2, lo, 0.0)))
        r_out[j, slot, BLOCK:RR, :] = packed.astype(BF)

    def r_copy(j, g, first, count):
        return copy(
            r_out.at[j, pl.ds(first, count)], r_in.at[j, pl.ds(first, count)],
            r_ss.at[j, g], r_rs.at[j, g], x_dev[j],
        )

    def serve(g, first, count):
        for j in (1, 2, 3):
            landed(q_in.at[j, pl.ds(first, count)], q_ss.at[j, g], q_rs.at[j, g])

        def one(j, carry):
            for a in range(count):
                attend(j, first + a)
            return carry

        lax.fori_loop(0, NX, one, 0)
        for j in (1, 2, 3):
            r_copy(j, g, first, count).start()

    def lse_of(ref, j, slot):
        tile = ref[j, slot, BLOCK:RR, :].astype(F32)
        return jnp.sum(tile, axis=0, keepdims=True)

    def column(row):
        return jnp.sum(jnp.where(diag, row, 0.0), axis=-1, keepdims=True)

    def merge(g, first, count):
        for j in (1, 2, 3):
            landed(r_in.at[j, pl.ds(first, count)], r_ss.at[j, g], r_rs.at[j, g])
        for a in range(count):
            slot = first + a
            rows = pl.ds(pl.multiple_of(block_of(slot) * BLOCK, BLOCK), BLOCK)
            for head, (ra, ja), (rb, jb) in (
                (x0, (r_out, 0), (r_in, 2)),
                (1 - x0, (r_in, 1), (r_in, 3)),
            ):
                gap = lse_of(rb, jb, slot) - lse_of(ra, ja, slot)
                wa = column(1.0 / (1.0 + jnp.exp(gap)))
                wb = column(1.0 / (1.0 + jnp.exp(-gap)))
                both = wa * ra[ja, slot, 0:BLOCK, :].astype(F32) + wb * rb[
                    jb, slot, 0:BLOCK, :
                ].astype(F32)
                out[rows, pl.ds(pl.multiple_of(head * HD, HD), HD)] = both.astype(BF)

    loads[4].wait()
    queries(0)
    for s in range(1, 7):
        for sub in range(2):
            for way in range(2):
                if z_needed(way, s, sub):
                    z_wait(way, s, sub)
                    if s < 6 and z_needed(way, s + 1, sub):
                        z_send(way, s, sub)
            if s <= 5:
                y_step(s - 1, sub)
        queries(s)
        if s == 5:
            for j in (1, 2, 3):
                landed(ids_v.at[j], i_ss.at[j], i_rs.at[j])
            to_smem = pltpu.make_async_copy(ids_v, ids_s, lsem.at[6])
            to_smem.start()
            to_smem.wait()
            for t in range(5):
                for way in range(2):
                    for sub in range(2):
                        if (way == 0 or t > 0) and y_needed(way, t, sub):
                            b_wait(way, t, sub)
            serve(0, 0, 1)

            def serve_pair(g, carry):
                serve(g, 2 * g - 1, 2)
                return carry

            lax.fori_loop(1, 5, serve_pair, 0)
    serve(5, 9, 2)
    serve(6, 11, 1)
    merge(0, 0, 1)

    def merge_pair(g, carry):
        merge(g, 2 * g - 1, 2)
        return carry

    lax.fori_loop(1, 6, merge_pair, 0)
    merge(6, 11, 1)

    for one in sent:
        one.wait_send()
    for j in (1, 2, 3):
        r_copy(j, 0, 0, 1).wait_send()
        r_copy(j, 6, 11, 1).wait_send()

        def pair_sent(g, carry):
            r_copy(j, g, 2 * g - 1, 2).wait_send()
            return carry

        lax.fori_loop(1, 6, pair_sent, 0)


def per_device(hidden, norm_gain, query_weight, key_weight, value_weight, bank, neighbour_ids):
    hbm = pl.BlockSpec(memory_space=pl.ANY)
    vmem = pl.BlockSpec(memory_space=pltpu.VMEM)
    dma = pltpu.SemaphoreType.DMA
    width = query_weight.shape[1]
    return pl.pallas_call(
        kernel,
        out_shape=jax.ShapeDtypeStruct((NZ * BLOCK, width), BF),
        in_specs=[hbm, vmem, hbm, hbm, hbm, hbm, hbm],
        out_specs=vmem,
        scratch_shapes=[
            pltpu.VMEM((BLOCK, D), BF),
            pltpu.VMEM((D, width), BF),
            pltpu.VMEM((D, width), BF),
            pltpu.VMEM((D, width), BF),
            pltpu.VMEM((ROWS, NBR, D), BF),
            pltpu.VMEM((NZ, BLOCK, D), BF),
            pltpu.VMEM((NY * 2 * 2 * ROWS, 2, NBR, HD), BF),
            pltpu.VMEM((ROWS, 2, NBR, HD), BF),
            pltpu.VMEM((NZ, BLOCK, HD), BF),
            pltpu.VMEM((NX, NZ, BLOCK, HD), BF),
            pltpu.VMEM((NX, NZ, RR, HD), BF),
            pltpu.VMEM((NX, NZ, RR, HD), BF),
            pltpu.VMEM((NX, NZ, 2), jnp.int32),
            pltpu.SMEM((NX, NZ, 2), jnp.int32),
            dma((7,)),
            dma((2, 6, 2)),
            dma((2, 6, 2)),
            dma((2, 4, 2)),
            dma((2, 4, 2)),
            dma((1,)),
            dma((1,)),
            dma((8, 2)),
            dma((8, 2)),
            dma((4, 7)),
            dma((4, 7)),
            dma((4, 7)),
            dma((4, 7)),
            dma((4,)),
            dma((4,)),
        ],
        compiler_params=pltpu.CompilerParams(
            collective_id=0, has_side_effects=True, vmem_limit_bytes=56 * 1024 * 1024
        ),
    )(
        hidden, norm_gain.reshape(1, D), query_weight, key_weight, value_weight, bank, neighbour_ids
    )


def solution(mesh):
    placed = (
        P(("db", "mp"), None),
        P(),
        P(None, "mp"),
        P(None, "mp"),
        P(None, "mp"),
        P("db", None, None),
        P("db", None),
    )
    return jax.shard_map(
        per_device, mesh=mesh, in_specs=placed, out_specs=P("db", "mp"), check_vma=False
    )
```

```python
import jax
import jax.numpy as jnp
from jax import lax
from jax.experimental import pallas as pl
from jax.experimental.pallas import tpu as pltpu
from jax.sharding import PartitionSpec as P

HD = 128
BLOCK = 64
NBR = 128
EPS = 1e-6
NX, NY, NZ = 4, 8, 12
D = 4096
ROWS = 4
NEG = -1e30
RR = 80
MESH = pl.DeviceIdType.MESH
BF = jnp.bfloat16
F32 = jnp.float32


def kernel(
    hidden, gain, wq, wk, wv, bank, ids, out,
    hid_v, wq_v, wk_v, wv_v, bank_v, zb, kv, kvs, qs, q_in, r_out, r_in, ids_v, ids_s,
    lsem, z_ss, z_rs, y_ss, y_rs, x_ss, x_rs, b_ss, b_rs, q_ss, q_rs, r_ss, r_rs, i_ss, i_rs,
):
    db = lax.axis_index("db")
    z = lax.axis_index("mp")
    c = db % 2
    x = (db // 2) % NX
    y = db // (2 * NX)
    x0 = x % 2
    x1 = x // 2

    def dev(yy, xx, cc, zz):
        return {"db": (yy * NX + xx) * 2 + cc, "mp": zz}

    xs = (x, x + 1 - 2 * x0, (x + 2) % NX, NX - 1 - x)
    z_dev = (dev(y, x, c, (z + 1) % NZ), dev(y, x, c, (z + NZ - 1) % NZ))
    y_dev = (dev((y + 1) % NY, x, c, z), dev((y + NY - 1) % NY, x, c, z))
    x_dev = tuple(dev(y, xx, c, z) for xx in xs)
    sib = dev(y, x, 1 - c, z)
    peers = z_dev + y_dev + x_dev[1:] + (sib,)

    loads = [
        pltpu.make_async_copy(a, b, lsem.at[n])
        for n, (a, b) in enumerate(
            ((hidden, hid_v), (bank, bank_v), (wk, wk_v), (wv, wv_v), (wq, wq_v), (ids, ids_v.at[0]))
        )
    ]
    for load in loads:
        load.start()
    barrier = pltpu.get_barrier_semaphore()
    for peer in peers:
        pl.semaphore_signal(barrier, inc=1, device_id=peer, device_id_type=MESH)

    def copy(src, dst, ss, rs, to):
        return pltpu.make_async_remote_copy(
            src_ref=src, dst_ref=dst, send_sem=ss, recv_sem=rs, device_id=to, device_id_type=MESH
        )

    sent = []

    def send(src, dst, ss, rs, to):
        one = copy(src, dst, ss, rs, to)
        one.start()
        sent.append(one)

    def landed(dst, ss, rs):
        copy(dst, dst, ss, rs, sib).wait_recv()

    loads[0].wait()

    def norm_rows(n, carry):
        rows = pl.ds(pl.multiple_of(n * 16, 16), 16)
        stream = hid_v[rows, :].astype(F32)
        factor = lax.rsqrt(jnp.mean(stream * stream, axis=-1, keepdims=True) + EPS)
        zb[0, rows, :] = (stream * factor * gain[...]).astype(BF)
        return carry

    lax.fori_loop(0, BLOCK // 16, norm_rows, 0)
    pl.semaphore_wait(barrier, len(peers))

    def z_part(slot, sub):
        return zb.at[slot, pl.ds(sub * 32, 32), :]

    def z_slot(way, s):
        return 0 if s == 0 else (11 if s == 6 else 2 * s - 1 + way)

    def z_send(way, s, sub):
        send(
            z_part(z_slot(way, s), sub), z_part(z_slot(way, s + 1), sub),
            z_ss.at[way, s, sub], z_rs.at[way, s, sub], z_dev[way],
        )

    def z_wait(way, s, sub):
        landed(z_part(z_slot(way, s), sub), z_ss.at[way, s - 1, sub], z_rs.at[way, s - 1, sub])

    def z_needed(way, s, sub):
        return s < 6 or sub == way

    for sub in range(2):
        for way in range(2):
            z_send(way, 0, sub)

    loads[5].wait()
    for j in (1, 2, 3):
        send(ids_v.at[0], ids_v.at[j], i_ss.at[j], i_rs.at[j], x_dev[j])

    def unit(yy, cc, bit):
        return ((yy * 2 + cc) * 2 + bit) * ROWS

    own = unit(y, c, x0)
    loads[1].wait()
    for which in range(2):
        loads[2 + which].wait()
        weight = (wk_v, wv_v)[which]

        def project(n, carry):
            got = jnp.dot(
                bank_v[pl.ds(n * 2, 2)].reshape(2 * NBR, D), weight[...], preferred_element_type=F32
            )
            low, high = got[:, :HD], got[:, HD:]
            mine = jnp.where(x0 == 0, low, high).astype(BF)
            other = jnp.where(x0 == 0, high, low).astype(BF)
            for a in range(2):
                kv[own + n * 2 + a, which] = mine[a * NBR : (a + 1) * NBR]
                kvs[n * 2 + a, which] = other[a * NBR : (a + 1) * NBR]
            return carry

        lax.fori_loop(0, ROWS // 2, project, 0)

    def y_at(way, s):
        return (y + NY - s) % NY if way == 0 else (y + s) % NY

    def kv_part(yy, cc, sub):
        return kv.at[pl.ds(unit(yy, cc, x0 if sub == 0 else 1 - x0), ROWS)]

    def y_send(way, s, sub):
        part = kv_part(y_at(way, s), c, sub)
        send(part, part, y_ss.at[way, s, sub], y_rs.at[way, s, sub], y_dev[way])

    def y_wait(way, s, sub):
        part = kv_part(y_at(way, s), c, sub)
        landed(part, y_ss.at[way, s - 1, sub], y_rs.at[way, s - 1, sub])

    def b_slot(way, s):
        return 0 if s == 0 else (7 if s == 4 else 2 * s - 1 + way)

    def b_send(way, s, sub):
        part = kv_part(y_at(way, s), c, sub)
        n = b_slot(way, s)
        send(part, part, b_ss.at[n, sub], b_rs.at[n, sub], sib)

    def b_wait(way, s, sub):
        n = b_slot(way, s)
        landed(kv_part(y_at(way, s), 1 - c, sub), b_ss.at[n, sub], b_rs.at[n, sub])

    send(kvs, kv.at[pl.ds(own, ROWS)], x_ss.at[0], x_rs.at[0], x_dev[1])
    for way in range(2):
        y_send(way, 0, 0)
    b_send(0, 0, 0)

    def y_needed(way, s, sub):
        return s < 4 or sub == way

    def y_step(s, sub):
        if s == 0:
            if sub == 1:
                landed(kv_part(y, c, 1), x_ss.at[0], x_rs.at[0])
                for way in range(2):
                    y_send(way, 0, 1)
                b_send(0, 0, 1)
            return
        for way in range(2):
            if y_needed(way, s, sub):
                y_wait(way, s, sub)
                if s < 4 and y_needed(way, s + 1, sub):
                    y_send(way, s, sub)
                b_send(way, s, sub)

    scale = HD ** (-0.5)

    def slots(g):
        return (0, 1) if g == 0 else ((11, 1) if g == 6 else (2 * g - 1, 2))

    def q_part(ref, g):
        first, count = slots(g)
        return ref.at[pl.ds(first, count)]

    def queries(g):
        first, count = slots(g)
        got = jnp.dot(
            zb[first : first + count].reshape(count * BLOCK, D), wq_v[...],
            preferred_element_type=F32,
        ) * scale
        low, high = got[:, :HD], got[:, HD:]
        mine = jnp.where(x0 == 0, low, high).astype(BF)
        other = jnp.where(x0 == 0, high, low).astype(BF)
        for a in range(count):
            q_in[0, first + a] = mine[a * BLOCK : (a + 1) * BLOCK]
            qs[first + a] = other[a * BLOCK : (a + 1) * BLOCK]
        for j in (2, 1, 3):
            src = q_part(q_in.at[0], g) if j == 2 else q_part(qs, g)
            send(src, q_part(q_in.at[j], g), q_ss.at[j, g], q_rs.at[j, g], x_dev[j])

    def block_of(slot):
        s = (slot + 1) // 2
        sign = 1 - 2 * (slot % 2)
        return (z + NZ + sign * s) % NZ

    diag = lax.broadcasted_iota(jnp.int32, (BLOCK, HD), 0) == lax.broadcasted_iota(
        jnp.int32, (BLOCK, HD), 1
    )
    row_no = lax.broadcasted_iota(jnp.int32, (16, HD), 0)

    lane = lax.broadcasted_iota(jnp.int32, (1, 2 * NBR), 1)

    def attend(items):
        loaded = []
        for j, slot in items:
            block = block_of(slot)
            rows, bias = [], []
            for k in range(2):
                nbr = ids_s[j, k, block]
                shard = nbr // ROWS
                col = (shard // 2) % NX
                rows.append(
                    ((shard // (2 * NX) * 2 + shard % 2) * 2 + col % 2) * ROWS + nbr % ROWS
                )
                bias.append(jnp.where(col // 2 == x1, 0.0, NEG))
            loaded.append((
                q_in[j, slot],
                jnp.concatenate([kv[rows[0], 0], kv[rows[1], 0]], axis=0),
                jnp.concatenate([kv[rows[0], 1], kv[rows[1], 1]], axis=0),
                jnp.where(lane < NBR, bias[0], bias[1]),
            ))
        scores = [
            lax.dot_general(q, keys, (((1,), (1,)), ((), ())), preferred_element_type=F32) + bias
            for q, keys, _, bias in loaded
        ]
        expo = [jnp.exp(s) for s in scores]
        denom = [jnp.sum(e, axis=-1, keepdims=True) for e in expo]
        down = [jnp.where(d > 1.0, 0.0625, 1.0) for d in denom]
        inverse = [jnp.where(d > 0.0, 1.0 / (d * w), 0.0) for d, w in zip(denom, down)]
        probs = [(e * w * v).astype(BF) for e, w, v in zip(expo, down, inverse)]
        parts = [
            jnp.dot(p, values, preferred_element_type=F32)
            for p, (_, _, values, _) in zip(probs, loaded)
        ]
        for (j, slot), part, d in zip(items, parts, denom):
            r_out[j, slot, 0:BLOCK, :] = part.astype(BF)
            total = jnp.sum(jnp.where(diag, d, 0.0), axis=0, keepdims=True)
            hi = total.astype(BF).astype(F32)
            mid = (total - hi).astype(BF).astype(F32)
            lo = total - hi - mid
            packed = jnp.where(
                row_no == 0, hi, jnp.where(row_no == 1, mid, jnp.where(row_no == 2, lo, 0.0))
            )
            r_out[j, slot, BLOCK:RR, :] = packed.astype(BF)

    def r_copy(j, g, first, count):
        return copy(
            r_out.at[j, pl.ds(first, count)], r_in.at[j, pl.ds(first, count)],
            r_ss.at[j, g], r_rs.at[j, g], x_dev[j],
        )

    def serve(g, first, count):
        for j in (1, 2, 3):
            landed(q_in.at[j, pl.ds(first, count)], q_ss.at[j, g], q_rs.at[j, g])

        attend([(j, first + a) for j in (1, 2, 3, 0) for a in range(count)])
        for j in (1, 2, 3):
            r_copy(j, g, first, count).start()

    def sum_of(ref, j, slot):
        return jnp.sum(ref[j, slot, BLOCK:RR, :].astype(F32), axis=0, keepdims=True)

    def column(row):
        return jnp.sum(jnp.where(diag, row, 0.0), axis=-1, keepdims=True)

    def merge(g, first, count):
        for j in (1, 2, 3):
            landed(r_in.at[j, pl.ds(first, count)], r_ss.at[j, g], r_rs.at[j, g])
        for a in range(count):
            slot = first + a
            rows = pl.ds(pl.multiple_of(block_of(slot) * BLOCK, BLOCK), BLOCK)
            for head, (ra, ja), (rb, jb) in (
                (x0, (r_out, 0), (r_in, 2)),
                (1 - x0, (r_in, 1), (r_in, 3)),
            ):
                la, lb = sum_of(ra, ja, slot), sum_of(rb, jb, slot)
                both = jnp.where(la + lb > 0.0, la + lb, 1.0)
                wa, wb = column(la / both), column(lb / both)
                mixed = wa * ra[ja, slot, 0:BLOCK, :].astype(F32) + wb * rb[
                    jb, slot, 0:BLOCK, :
                ].astype(F32)
                out[rows, pl.ds(pl.multiple_of(head * HD, HD), HD)] = mixed.astype(BF)

    loads[4].wait()
    queries(0)
    for s in range(1, 7):
        for sub in range(2):
            for way in range(2):
                if z_needed(way, s, sub):
                    z_wait(way, s, sub)
                    if s < 6 and z_needed(way, s + 1, sub):
                        z_send(way, s, sub)
            if s <= 4:
                y_step(s - 1, sub)
        queries(s)
        if s == 4:
            for j in (1, 2, 3):
                landed(ids_v.at[j], i_ss.at[j], i_rs.at[j])
            to_smem = pltpu.make_async_copy(ids_v, ids_s, lsem.at[6])
            to_smem.start()
            to_smem.wait()
            for sub in range(2):
                y_step(4, sub)
            for t in range(5):
                for way in range(2):
                    for sub in range(2):
                        if (way == 0 or t > 0) and y_needed(way, t, sub):
                            b_wait(way, t, sub)
            serve(0, 0, 1)

            def serve_pair(g, carry):
                serve(g, 2 * g - 1, 2)
                return carry

            lax.fori_loop(1, 4, serve_pair, 0)
    serve(4, 7, 2)
    serve(5, 9, 2)
    serve(6, 11, 1)
    merge(0, 0, 1)

    def merge_pair(g, carry):
        merge(g, 2 * g - 1, 2)
        return carry

    lax.fori_loop(1, 6, merge_pair, 0)
    merge(6, 11, 1)

    for one in sent:
        one.wait_send()
    for j in (1, 2, 3):
        r_copy(j, 0, 0, 1).wait_send()
        r_copy(j, 6, 11, 1).wait_send()

        def pair_sent(g, carry):
            r_copy(j, g, 2 * g - 1, 2).wait_send()
            return carry

        lax.fori_loop(1, 6, pair_sent, 0)


def per_device(hidden, norm_gain, query_weight, key_weight, value_weight, bank, neighbour_ids):
    hbm = pl.BlockSpec(memory_space=pl.ANY)
    vmem = pl.BlockSpec(memory_space=pltpu.VMEM)
    dma = pltpu.SemaphoreType.DMA
    width = query_weight.shape[1]
    return pl.pallas_call(
        kernel,
        out_shape=jax.ShapeDtypeStruct((NZ * BLOCK, width), BF),
        in_specs=[hbm, vmem, hbm, hbm, hbm, hbm, hbm],
        out_specs=vmem,
        scratch_shapes=[
            pltpu.VMEM((BLOCK, D), BF),
            pltpu.VMEM((D, width), BF),
            pltpu.VMEM((D, width), BF),
            pltpu.VMEM((D, width), BF),
            pltpu.VMEM((ROWS, NBR, D), BF),
            pltpu.VMEM((NZ, BLOCK, D), BF),
            pltpu.VMEM((NY * 2 * 2 * ROWS, 2, NBR, HD), BF),
            pltpu.VMEM((ROWS, 2, NBR, HD), BF),
            pltpu.VMEM((NZ, BLOCK, HD), BF),
            pltpu.VMEM((NX, NZ, BLOCK, HD), BF),
            pltpu.VMEM((NX, NZ, RR, HD), BF),
            pltpu.VMEM((NX, NZ, RR, HD), BF),
            pltpu.VMEM((NX, 2, NZ), jnp.int32),
            pltpu.SMEM((NX, 2, NZ), jnp.int32),
            dma((7,)),
            dma((2, 6, 2)),
            dma((2, 6, 2)),
            dma((2, 4, 2)),
            dma((2, 4, 2)),
            dma((1,)),
            dma((1,)),
            dma((8, 2)),
            dma((8, 2)),
            dma((4, 7)),
            dma((4, 7)),
            dma((4, 7)),
            dma((4, 7)),
            dma((4,)),
            dma((4,)),
        ],
        compiler_params=pltpu.CompilerParams(
            collective_id=0, has_side_effects=True, vmem_limit_bytes=56 * 1024 * 1024
        ),
    )(
        hidden, norm_gain.reshape(1, D), query_weight, key_weight, value_weight, bank, neighbour_ids.T
    )


def solution(mesh):
    placed = (
        P(("db", "mp"), None),
        P(),
        P(None, "mp"),
        P(None, "mp"),
        P(None, "mp"),
        P("db", None, None),
        P("db", None),
    )
    return jax.shard_map(
        per_device, mesh=mesh, in_specs=placed, out_specs=P("db", "mp"), check_vma=False
    )
```

```python
import jax
import jax.numpy as jnp
from jax import lax
from jax.experimental import pallas as pl
from jax.experimental.pallas import tpu as pltpu
from jax.sharding import PartitionSpec as P

HD = 128
BLOCK = 64
NBR = 128
EPS = 1e-6
NX, NY, NZ = 4, 8, 12
D = 4096
ROWS = 4
NEG = -1e30
RR = 80
MESH = pl.DeviceIdType.MESH
BF = jnp.bfloat16
F32 = jnp.float32


GROUPS = ((0, 1), (1, 2), (3, 2), (5, 1), (6, 2), (8, 2), (10, 2))
HALF = NZ // 2


def kernel(
    hidden, gain, wq, wk, wv, bank, ids, out,
    hid_v, wq_v, w2_v, wk_v, wv_v, bank_v, zb, kv, kvs, qq, q2, q_in, r_out, r_in, ids_v, ids_s,
    lsem, s_sem, z_rs, y_rs, x_rs, b_rs, q_rs, r_rs, i_rs, w0_rs, wy_rs, wx_rs, wb_rs, f_rs,
    out_v, o_sem,
):
    db = lax.axis_index("db")
    z = lax.axis_index("mp")
    c = db % 2
    x = (db // 2) % NX
    y = db // (2 * NX)
    x0 = x % 2
    x1 = x // 2
    turn = 1 - 2 * c

    def dev(yy, xx, cc, zz):
        return {"db": (yy * NX + xx) * 2 + cc, "mp": zz}

    xs = (x, x + 1 - 2 * x0, (x + 2) % NX, NX - 1 - x)
    z_dev = (dev(y, x, c, (z + NZ - turn) % NZ), dev(y, x, c, (z + NZ + turn) % NZ))
    far = dev(y, x, c, (z + HALF) % NZ)
    y_dev = tuple(dev((y + d) % NY, x, c, z) for d in range(NY))
    x_dev = tuple(dev(y, xx, c, z) for xx in xs)
    ring = (dev(y, (x + 1) % NX, c, z), dev(y, (x + NX - 1) % NX, c, z))
    sib = dev(y, x, 1 - c, z)
    peers = z_dev + (far,) + y_dev[1:] + x_dev[1:] + (sib,)

    loads = [
        pltpu.make_async_copy(a, b, lsem.at[n])
        for n, (a, b) in enumerate(
            ((hidden, hid_v), (wq, wq_v), (bank, bank_v), (wk, wk_v), (wv, wv_v), (ids, ids_v.at[0]))
        )
    ]
    for load in loads:
        load.start()
    barrier = pltpu.get_barrier_semaphore()
    for peer in peers:
        pl.semaphore_signal(barrier, inc=1, device_id=peer, device_id_type=MESH)

    def copy(src, dst, ss, rs, to):
        return pltpu.make_async_remote_copy(
            src_ref=src, dst_ref=dst, send_sem=ss, recv_sem=rs, device_id=to, device_id_type=MESH
        )

    def send(src, dst, family, rs, to):
        copy(src, dst, s_sem.at[family], rs, to).start()

    def landed(dst, rs):
        copy(dst, dst, s_sem.at[0], rs, sib).wait_recv()

    def all_sent(like, family):
        copy(like, like, s_sem.at[family], s_sem.at[family], sib).wait_send()

    loads[0].wait()

    def norm_rows(n, carry):
        rows = pl.ds(pl.multiple_of(n * 16, 16), 16)
        stream = hid_v[rows, :].astype(F32)
        factor = lax.rsqrt(jnp.mean(stream * stream, axis=-1, keepdims=True) + EPS)
        zb[0, rows, :] = (stream * factor * gain[...]).astype(BF)
        return carry

    lax.fori_loop(0, BLOCK // 16, norm_rows, 0)
    loads[1].wait()
    pl.semaphore_wait(barrier, len(peers))

    def w_rows(first, count):
        return w2_v.at[pl.ds(pl.multiple_of(first, 64), count)]

    def w_slice(yy):
        return w_rows(x * 1024 + c * 512 + yy * 64, 64)

    send(
        wq_v.at[pl.ds(pl.multiple_of(x * 1024 + c * 512 + y * 64, 64), 64)], w_slice(y),
        0, w0_rs.at[0], far,
    )

    def w_along_y():
        landed(w_slice(y), w0_rs.at[0])
        for d in (1, 7, 2, 6, 3, 5, 4):
            send(w_slice(y), w_slice(y), 1, wy_rs.at[0], y_dev[d])

    def w_block(xx, cc):
        return w_rows(xx * 1024 + cc * 512, 512)

    def w_half(xx, cc, half):
        return w_rows(xx * 1024 + cc * 512 + half * 256, 256)

    def w_along_x():
        landed(w2_v.at[pl.ds(0, 64 * (NY - 1))], wy_rs.at[0])
        own_block = w_block(x, c)
        for way in range(2):
            send(own_block, own_block, 2, wx_rs.at[way, 0], ring[way])
        send(own_block, own_block, 3, wb_rs.at[0], sib)

    def w_from(way):
        return (x + NX - 1) % NX if way == 0 else (x + 1) % NX

    def w_on():
        for way in range(2):
            block = w_block(w_from(way), c)
            landed(block, wx_rs.at[way, 0])
            half = w_half(w_from(way), c, way)
            send(half, half, 2, wx_rs.at[way, 1], ring[way])
            send(block, block, 3, wb_rs.at[0], sib)

    def w_last():
        for way in range(2):
            half = w_half((x + 2) % NX, c, way)
            landed(half, wx_rs.at[way, 1])
            send(half, half, 3, wb_rs.at[0], sib)

    def w_whole():
        landed(w2_v.at[pl.ds(0, D // 2)], wb_rs.at[0])

    STEPS = (3, 2)

    def z_part(slot, sub):
        return zb.at[slot, pl.ds(sub * 32, 32), :]

    def z_slot(way, s):
        return 0 if s == 0 else 2 * s - 1 + way

    def z_send(way, s, sub):
        send(
            z_part(z_slot(way, s), sub), z_part(z_slot(way, s + 1), sub),
            4, z_rs.at[way, s, sub], z_dev[way],
        )

    def z_step(s, sub):
        for way in range(2):
            if s <= STEPS[way]:
                landed(z_part(z_slot(way, s), sub), z_rs.at[way, s - 1, sub])
                if s < STEPS[way]:
                    z_send(way, s, sub)

    for sub in range(2):
        for way in range(2):
            z_send(way, 0, sub)

    loads[5].wait()
    for j in (1, 2, 3):
        send(ids_v.at[0], ids_v.at[j], 5, i_rs.at[0], x_dev[j])

    def unit(yy, cc, bit):
        return ((yy * 2 + cc) * 2 + bit) * ROWS

    own = unit(y, c, x0)

    def project(which):
        weight = (wk_v, wv_v)[which]

        def rows_of(n, carry):
            got = jnp.dot(
                bank_v[pl.ds(n * 2, 2)].reshape(2 * NBR, D), weight[...], preferred_element_type=F32
            )
            low, high = got[:, :HD], got[:, HD:]
            mine = jnp.where(x0 == 0, low, high).astype(BF)
            other = jnp.where(x0 == 0, high, low).astype(BF)
            for a in range(2):
                kv[which, own + n * 2 + a] = mine[a * NBR : (a + 1) * NBR]
                kvs[which, n * 2 + a] = other[a * NBR : (a + 1) * NBR]
            return carry

        lax.fori_loop(0, ROWS // 2, rows_of, 0)

    def y_at(way, s):
        return (y + NY - s) % NY if way == 0 else (y + s) % NY

    def kv_part(yy, cc, sub):
        return kv.at[sub % 2, pl.ds(unit(yy, cc, x0 if sub < 2 else 1 - x0), ROWS)]

    def y_send(way, s, sub):
        part = kv_part(y_at(way, s), c, sub)
        send(part, part, 6, y_rs.at[way, s, sub], y_dev[1 if way == 0 else NY - 1])

    def b_send(way, s, sub):
        part = kv_part(y_at(way, s), c, sub)
        send(part, part, 7, b_rs.at[0], sib)

    def y_needed(way, s, sub):
        return s < 4 or sub // 2 == way

    def y_first(sub):
        for way in range(2):
            y_send(way, 0, sub)
        b_send(0, 0, sub)

    def y_step(s, *subs, ways=(0, 1)):
        for sub in subs:
            for way in ways:
                if y_needed(way, s, sub):
                    part = kv_part(y_at(way, s), c, sub)
                    landed(part, y_rs.at[way, s - 1, sub])
                    if s < 4 and y_needed(way, s + 1, sub):
                        y_send(way, s, sub)
                    b_send(way, s, sub)

    def neighbour(which):
        landed(kv_part(y, c, 2 + which), x_rs.at[which])
        y_first(2 + which)

    scale = HD ** (-0.5)

    def store_queries(got, ref, first, count):
        got = got * scale
        low, high = got[:, :HD], got[:, HD:]
        mine = jnp.where(x0 == 0, low, high).astype(BF)
        other = jnp.where(x0 == 0, high, low).astype(BF)
        for a in range(count):
            ref[first + a, 0] = mine[a * BLOCK : (a + 1) * BLOCK]
            ref[first + a, 1] = other[a * BLOCK : (a + 1) * BLOCK]

    def rows_of_slots(first, count):
        return zb[first : first + count].reshape(count * BLOCK, D)

    def q_along_x(g):
        first, count = GROUPS[g]
        for j in (2, 1, 3):
            send(
                qq.at[pl.ds(first, count), 0 if j == 2 else 1], q_in.at[j, pl.ds(first, count)],
                9, q_rs.at[g], x_dev[j],
            )

    def queries(g):
        first, count = GROUPS[g]
        got = jnp.dot(rows_of_slots(first, count), wq_v[...], preferred_element_type=F32)
        store_queries(got, qq, first, count)
        q_along_x(g)

    def far_queries(n):
        got = jnp.dot(rows_of_slots(2 * n, 2), w2_v[...], preferred_element_type=F32)
        store_queries(got, q2, 2 * n, 2)
        send(
            q2.at[pl.ds(2 * n, 2)], qq.at[pl.ds(HALF + 2 * n, 2)], 10, f_rs.at[n], far
        )

    def relay(n):
        landed(qq.at[pl.ds(HALF + 2 * n, 2)], f_rs.at[n])
        q_along_x(4 + n)

    def block_of(slot):
        u = slot % HALF
        sign = turn * (2 * (u % 2) - 1)
        return (z + NZ + HALF * (slot // HALF) + sign * ((u + 1) // 2)) % NZ

    diag = lax.broadcasted_iota(jnp.int32, (BLOCK, HD), 0) == lax.broadcasted_iota(
        jnp.int32, (BLOCK, HD), 1
    )
    row_no = lax.broadcasted_iota(jnp.int32, (16, HD), 0)

    lane = lax.broadcasted_iota(jnp.int32, (1, 2 * NBR), 1)

    def attend(items):
        loaded = []
        for j, slot in items:
            block = block_of(slot)
            rows, bias = [], []
            for k in range(2):
                nbr = ids_s[j, k, block]
                shard = nbr // ROWS
                col = (shard // 2) % NX
                rows.append(
                    ((shard // (2 * NX) * 2 + shard % 2) * 2 + col % 2) * ROWS + nbr % ROWS
                )
                bias.append(jnp.where(col // 2 == x1, 0.0, NEG))
            loaded.append((
                qq[slot, 0] if j == 0 else q_in[j, slot],
                jnp.concatenate([kv[0, rows[0]], kv[0, rows[1]]], axis=0),
                jnp.concatenate([kv[1, rows[0]], kv[1, rows[1]]], axis=0),
                jnp.where(lane < NBR, bias[0], bias[1]),
            ))
        scores = [
            lax.dot_general(q, keys, (((1,), (1,)), ((), ())), preferred_element_type=F32) + bias
            for q, keys, _, bias in loaded
        ]
        expo = [jnp.exp(s) for s in scores]
        denom = [jnp.sum(e, axis=-1, keepdims=True) for e in expo]
        down = [jnp.where(d > 1.0, 0.0625, 1.0) for d in denom]
        inverse = [jnp.where(d > 0.0, 1.0 / (d * w), 0.0) for d, w in zip(denom, down)]
        probs = [(e * w * v).astype(BF) for e, w, v in zip(expo, down, inverse)]
        parts = [
            jnp.dot(p, values, preferred_element_type=F32)
            for p, (_, _, values, _) in zip(probs, loaded)
        ]
        for (j, slot), part, d in zip(items, parts, denom):
            r_out[j, slot, 0:BLOCK, :] = part.astype(BF)
            total = jnp.sum(jnp.where(diag, d, 0.0), axis=0, keepdims=True)
            hi = total.astype(BF).astype(F32)
            mid = (total - hi).astype(BF).astype(F32)
            lo = total - hi - mid
            packed = jnp.where(
                row_no == 0, hi, jnp.where(row_no == 1, mid, jnp.where(row_no == 2, lo, 0.0))
            )
            r_out[j, slot, BLOCK:RR, :] = packed.astype(BF)

    def r_copy(j, g, first, count):
        return copy(
            r_out.at[j, pl.ds(first, count)], r_in.at[j, pl.ds(first, count)],
            s_sem.at[11], r_rs.at[g], x_dev[j],
        )

    def serve(parts):
        for g, first, count in parts:
            landed(q_in.at[pl.ds(1, 3), pl.ds(first, count)], q_rs.at[g])
        attend([
            (j, first + a) for j in (1, 2, 3, 0) for _, first, count in parts for a in range(count)
        ])
        for g, first, count in parts:
            for j in (1, 2, 3):
                r_copy(j, g, first, count).start()

    ones = jnp.ones((16, HD), BF)

    def sum_of(ref, j, slot):
        spread = lax.dot_general(
            ref[j, slot, BLOCK:RR, :], ones, (((0,), (0,)), ((), ())), preferred_element_type=F32
        )
        return spread[:BLOCK]

    def out_copy(slot):
        rows = pl.ds(pl.multiple_of(block_of(slot) * BLOCK, BLOCK), BLOCK)
        return pltpu.make_async_copy(out_v.at[slot], out.at[rows], o_sem.at[0])

    def merge(parts):
        for g, first, count in parts:
            landed(r_in.at[pl.ds(1, 3), pl.ds(first, count)], r_rs.at[g])
        slots = [first + a for _, first, count in parts for a in range(count)]
        todo = [
            (slot, head, pair)
            for slot in slots
            for head, pair in ((x0, ((r_out, 0), (r_in, 2))), (1 - x0, ((r_in, 1), (r_in, 3))))
        ]
        sums = [[sum_of(ref, j, slot) for ref, j in pair] for slot, _, pair in todo]
        vals = [
            [ref[j, slot, 0:BLOCK, :].astype(F32) for ref, j in pair] for slot, _, pair in todo
        ]
        for (slot, head, _), (la, lb), (va, vb) in zip(todo, sums, vals):
            both = jnp.where(la + lb > 0.0, la + lb, 1.0)
            mixed = (la / both) * va + (lb / both) * vb
            out_v[slot, :, pl.ds(pl.multiple_of(head * HD, HD), HD)] = mixed.astype(BF)
        for slot in slots:
            out_copy(slot).start()

    loads[2].wait()
    loads[3].wait()
    project(0)
    y_first(0)
    send(kvs.at[0], kv.at[0, pl.ds(own, ROWS)], 8, x_rs.at[0], x_dev[1])
    loads[4].wait()
    project(1)
    y_first(1)
    send(kvs.at[1], kv.at[1, pl.ds(own, ROWS)], 8, x_rs.at[1], x_dev[1])
    queries(0)
    w_along_y()
    z_step(1, 0)
    w_along_x()
    y_step(1, 0)
    neighbour(0)
    y_step(1, 1)
    neighbour(1)
    landed(ids_v.at[pl.ds(1, 3)], i_rs.at[0])
    to_smem = pltpu.make_async_copy(ids_v, ids_s, lsem.at[6])
    to_smem.start()
    z_step(1, 1)
    queries(1)
    z_step(2, 0)
    w_on()
    w_last()
    z_step(2, 1)
    queries(2)
    y_step(1, 2, 3)
    y_step(2, 0, 1)
    w_whole()
    far_queries(0)
    far_queries(1)
    z_step(3, 0)
    z_step(3, 1)
    queries(3)
    far_queries(2)
    y_step(2, 2, 3)
    y_step(3, 0, 1)
    relay(0)
    relay(1)
    y_step(3, 2, 3, ways=(1,))
    relay(2)
    y_step(3, 2, 3, ways=(0,))
    to_smem.wait()
    y_step(4, 0, 2, 1, 3)
    landed(kv.at[0], b_rs.at[0])

    serve([(0, 0, 1), (3, 5, 1)])

    def serve_near(n, carry):
        serve([(1 + n, 1 + 2 * n, 2)])
        return carry

    def serve_away(n, carry):
        serve([(4 + n, HALF + 2 * n, 2)])
        return carry

    lax.fori_loop(0, 2, serve_near, 0)
    lax.fori_loop(0, 3, serve_away, 0)
    merge([(0, 0, 1), (3, 5, 1)])

    def merge_near(n, carry):
        merge([(1 + n, 1 + 2 * n, 2)])
        return carry

    def merge_away(n, carry):
        merge([(4 + n, HALF + 2 * n, 2)])
        return carry

    lax.fori_loop(0, 2, merge_near, 0)
    lax.fori_loop(0, 3, merge_away, 0)

    for family, like in enumerate((
        w2_v.at[pl.ds(0, 64)],
        w2_v.at[pl.ds(0, 64 * (NY - 1))],
        w2_v.at[pl.ds(0, 1536)],
        w2_v.at[pl.ds(0, D // 2)],
        zb.at[pl.ds(0, 5)],
        ids_v.at[pl.ds(1, 3)],
        kv.at[0, pl.ds(0, 112)],
        kv.at[0],
        kvs,
        q_in.at[pl.ds(1, 3)],
        q2,
        r_in.at[pl.ds(1, 3)],
    )):
        all_sent(like, family)
    pltpu.make_async_copy(out_v, out_v, o_sem.at[0]).wait()


def per_device(hidden, norm_gain, query_weight, key_weight, value_weight, bank, neighbour_ids):
    hbm = pl.BlockSpec(memory_space=pl.ANY)
    vmem = pl.BlockSpec(memory_space=pltpu.VMEM)
    dma = pltpu.SemaphoreType.DMA
    width = query_weight.shape[1]
    return pl.pallas_call(
        kernel,
        out_shape=jax.ShapeDtypeStruct((NZ * BLOCK, width), BF),
        in_specs=[hbm, vmem, hbm, hbm, hbm, hbm, hbm],
        out_specs=hbm,
        scratch_shapes=[
            pltpu.VMEM((BLOCK, D), BF),
            pltpu.VMEM((D, width), BF),
            pltpu.VMEM((D, width), BF),
            pltpu.VMEM((D, width), BF),
            pltpu.VMEM((D, width), BF),
            pltpu.VMEM((ROWS, NBR, D), BF),
            pltpu.VMEM((HALF, BLOCK, D), BF),
            pltpu.VMEM((2, NY * 2 * 2 * ROWS, NBR, HD), BF),
            pltpu.VMEM((2, ROWS, NBR, HD), BF),
            pltpu.VMEM((NZ, 2, BLOCK, HD), BF),
            pltpu.VMEM((HALF, 2, BLOCK, HD), BF),
            pltpu.VMEM((NX, NZ, BLOCK, HD), BF),
            pltpu.VMEM((NX, NZ, RR, HD), BF),
            pltpu.VMEM((NX, NZ, RR, HD), BF),
            pltpu.VMEM((NX, 2, NZ), jnp.int32),
            pltpu.SMEM((NX, 2, NZ), jnp.int32),
            dma((7,)),
            dma((12,)),
            dma((2, 3, 2)),
            dma((2, 4, 4)),
            dma((2,)),
            dma((1,)),
            dma((7,)),
            dma((7,)),
            dma((1,)),
            dma((1,)),
            dma((1,)),
            dma((2, 2)),
            dma((1,)),
            dma((3,)),
            pltpu.VMEM((NZ, BLOCK, width), BF),
            dma((1,)),
        ],
        compiler_params=pltpu.CompilerParams(
            collective_id=0, has_side_effects=True, vmem_limit_bytes=56 * 1024 * 1024
        ),
    )(
        hidden, norm_gain.reshape(1, D), query_weight, key_weight, value_weight, bank, neighbour_ids.T
    )


def solution(mesh):
    placed = (
        P(("db", "mp"), None),
        P(),
        P(None, "mp"),
        P(None, "mp"),
        P(None, "mp"),
        P("db", None, None),
        P("db", None),
    )
    return jax.shard_map(
        per_device, mesh=mesh, in_specs=placed, out_specs=P("db", "mp"), check_vma=False
    )
```

```python
import jax
import jax.numpy as jnp
from jax import lax
from jax.experimental import pallas as pl
from jax.experimental.pallas import tpu as pltpu
from jax.sharding import PartitionSpec as P

HD = 128
BLOCK = 64
NBR = 128
EPS = 1e-6
NX, NY, NZ = 4, 8, 12
D = 4096
ROWS = 4
NEG = -1e30
RR = 144
MESH = pl.DeviceIdType.MESH
BF = jnp.bfloat16
F32 = jnp.float32


GROUPS = ((0, 1), (1, 2), (3, 2), (5, 1), (6, 2), (8, 2), (10, 2))
HALF = NZ // 2


def kernel(
    hidden, gain, wq, wk, wv, bank, ids, out,
    hid_v, wq_v, w2_v, wk_v, wv_v, bank_v, zb, kv, kvs, qq, q2, q_in, r_out, r_in, ids_v, ids_s,
    lsem, s_sem, z_rs, y_rs, x_rs, b_rs, q_rs, r_rs, i_rs, w0_rs, wy_rs, wx_rs, wb_rs, f_rs,
    out_v, o_sem,
):
    db = lax.axis_index("db")
    z = lax.axis_index("mp")
    c = db % 2
    x = (db // 2) % NX
    y = db // (2 * NX)
    x0 = x % 2
    x1 = x // 2
    turn = 1 - 2 * c

    def dev(yy, xx, cc, zz):
        return {"db": (yy * NX + xx) * 2 + cc, "mp": zz}

    xs = (x, x + 1 - 2 * x0, (x + 2) % NX, NX - 1 - x)
    z_dev = (dev(y, x, c, (z + NZ - turn) % NZ), dev(y, x, c, (z + NZ + turn) % NZ))
    far = dev(y, x, c, (z + HALF) % NZ)
    y_dev = (dev((y + 1) % NY, x, c, z), dev((y + NY - 1) % NY, x, c, z))
    away = 2 * (y % 2) - 1
    y_three = tuple(dev((y + NY + away * d) % NY, x, c, z) for d in (1, 2, 3))
    x_dev = tuple(dev(y, xx, c, z) for xx in xs)
    ring = (dev(y, (x + 1) % NX, c, z), dev(y, (x + NX - 1) % NX, c, z))
    sib = dev(y, x, 1 - c, z)
    peers = z_dev + (far,) + tuple(dev((y + d) % NY, x, c, z) for d in (1, 2, 3, 5, 6, 7)) + x_dev[1:] + (sib,)

    half = ROWS // 2
    loads = [
        pltpu.make_async_copy(a, b, lsem.at[n])
        for n, (a, b) in enumerate((
            (hidden, hid_v),
            (ids, ids_v.at[0]),
            (wk, wk_v),
            (bank.at[pl.ds(0, half)], bank_v.at[pl.ds(0, half)]),
            (bank.at[pl.ds(half, half)], bank_v.at[pl.ds(half, half)]),
            (wv, wv_v),
            (wq, wq_v),
        ))
    ]
    for load in loads:
        load.start()
    barrier = pltpu.get_barrier_semaphore()
    for peer in peers:
        pl.semaphore_signal(barrier, inc=1, device_id=peer, device_id_type=MESH)

    def copy(src, dst, ss, rs, to):
        return pltpu.make_async_remote_copy(
            src_ref=src, dst_ref=dst, send_sem=ss, recv_sem=rs, device_id=to, device_id_type=MESH
        )

    def send(src, dst, family, rs, to):
        copy(src, dst, s_sem.at[family], rs, to).start()

    def landed(dst, rs):
        copy(dst, dst, s_sem.at[0], rs, sib).wait_recv()

    def all_sent(like, family):
        copy(like, like, s_sem.at[family], s_sem.at[family], sib).wait_send()

    def norm():
        def norm_rows(n, carry):
            rows = pl.ds(pl.multiple_of(n * 16, 16), 16)
            stream = hid_v[rows, :].astype(F32)
            factor = lax.rsqrt(jnp.mean(stream * stream, axis=-1, keepdims=True) + EPS)
            zb[0, rows, :] = (stream * factor * gain[...]).astype(BF)
            return carry

        lax.fori_loop(0, BLOCK // 16, norm_rows, 0)

    def w_rows(first, count):
        return w2_v.at[pl.ds(pl.multiple_of(first, 64), count)]

    def w_slice(yy):
        return w_rows(x * 1024 + c * 512 + yy // 2 * 128, 128)

    def w_far():
        first = pl.multiple_of(x * 1024 + c * 512 + y // 2 * 128, 128)
        send(wq.at[pl.ds(first, 128)], w_slice(y), 0, w0_rs.at[0], far)

    def w_along_y():
        landed(w_slice(y), w0_rs.at[0])
        for to in y_three:
            send(w_slice(y), w_slice(y), 1, wy_rs.at[0], to)

    def w_block(xx, cc):
        return w_rows(xx * 1024 + cc * 512, 512)

    def w_half(xx, cc, half):
        return w_rows(xx * 1024 + cc * 512 + half * 256, 256)

    def w_along_x():
        landed(w2_v.at[pl.ds(0, 3 * 128)], wy_rs.at[0])
        own_block = w_block(x, c)
        for way in range(2):
            send(own_block, own_block, 2, wx_rs.at[way, 0], ring[way])
        send(own_block, own_block, 3, wb_rs.at[0], sib)

    def w_from(way):
        return (x + NX - 1) % NX if way == 0 else (x + 1) % NX

    def w_on():
        for way in range(2):
            block = w_block(w_from(way), c)
            landed(block, wx_rs.at[way, 0])
            half = w_half(w_from(way), c, way)
            send(half, half, 2, wx_rs.at[way, 1], ring[way])
            send(block, block, 3, wb_rs.at[0], sib)

    def w_last():
        for way in range(2):
            half = w_half((x + 2) % NX, c, way)
            landed(half, wx_rs.at[way, 1])
            send(half, half, 3, wb_rs.at[0], sib)

    def w_whole():
        landed(w2_v.at[pl.ds(0, D // 2)], wb_rs.at[0])

    STEPS = (3, 2)

    def z_part(slot, sub):
        return zb.at[slot, pl.ds(sub * 32, 32), :]

    def z_slot(way, s):
        return 0 if s == 0 else 2 * s - 1 + way

    def z_send(way, s, sub):
        send(
            z_part(z_slot(way, s), sub), z_part(z_slot(way, s + 1), sub),
            4, z_rs.at[way, s, sub], z_dev[way],
        )

    def z_step(s, sub):
        for way in range(2):
            if s <= STEPS[way]:
                landed(z_part(z_slot(way, s), sub), z_rs.at[way, s - 1, sub])
                if s < STEPS[way]:
                    z_send(way, s, sub)

    def z_first():
        for sub in range(2):
            for way in range(2):
                z_send(way, 0, sub)

    def unit(yy, cc, bit):
        return ((yy * 2 + cc) * 2 + bit) * ROWS

    own = unit(y, c, x0)

    def project(which, n):
        got = jnp.dot(
            bank_v[pl.ds(n * half, half)].reshape(half * NBR, D), (wk_v, wv_v)[which][...],
            preferred_element_type=F32,
        )
        low, high = got[:, :HD], got[:, HD:]
        mine = jnp.where(x0 == 0, low, high).astype(BF)
        other = jnp.where(x0 == 0, high, low).astype(BF)
        for a in range(half):
            kv[which, own + n * half + a] = mine[a * NBR : (a + 1) * NBR]
            kvs[which, n * half + a] = other[a * NBR : (a + 1) * NBR]

    def pass_on(which, n):
        part = kv.at[which, pl.ds(own + n * half, half)]
        for way in range(2):
            send(part, part, 6, y_rs.at[way, 0, which], y_dev[way])
        send(kvs.at[which, pl.ds(n * half, half)], part, 8, x_rs.at[which], x_dev[1])
        send(part, part, 7, b_rs.at[0], sib)

    def y_at(way, s):
        return (y + NY - s) % NY if way == 0 else (y + s) % NY

    def kv_part(yy, cc, sub):
        return kv.at[sub % 2, pl.ds(unit(yy, cc, x0 if sub < 2 else 1 - x0), ROWS)]

    def y_send(way, s, sub):
        part = kv_part(y_at(way, s), c, sub)
        send(part, part, 6, y_rs.at[way, s, sub], y_dev[way])

    def b_send(way, s, sub):
        part = kv_part(y_at(way, s), c, sub)
        send(part, part, 7, b_rs.at[0], sib)

    def y_needed(way, s, sub):
        return s < 4 or sub // 2 == way

    def y_first(sub):
        for way in range(2):
            y_send(way, 0, sub)
        b_send(0, 0, sub)

    def y_step(s, *subs, ways=(0, 1)):
        for sub in subs:
            for way in ways:
                if y_needed(way, s, sub):
                    part = kv_part(y_at(way, s), c, sub)
                    landed(part, y_rs.at[way, s - 1, sub])
                    if s < 4 and y_needed(way, s + 1, sub):
                        y_send(way, s, sub)
                    b_send(way, s, sub)

    def neighbour(which):
        landed(kv_part(y, c, 2 + which), x_rs.at[which])
        y_first(2 + which)

    scale = HD ** (-0.5)

    def store_queries(got, ref, first, count):
        got = got * scale
        low, high = got[:, :HD], got[:, HD:]
        mine = jnp.where(x0 == 0, low, high).astype(BF)
        other = jnp.where(x0 == 0, high, low).astype(BF)
        for a in range(count):
            ref[first + a, 0] = mine[a * BLOCK : (a + 1) * BLOCK]
            ref[first + a, 1] = other[a * BLOCK : (a + 1) * BLOCK]

    def rows_of_slots(first, count):
        return zb[first : first + count].reshape(count * BLOCK, D)

    def q_along_x(g):
        first, count = GROUPS[g]
        for j in (2, 1, 3):
            send(
                qq.at[pl.ds(first, count), 0 if j == 2 else 1], q_in.at[j, pl.ds(first, count)],
                9, q_rs.at[g], x_dev[j],
            )

    def queries(g):
        first, count = GROUPS[g]
        got = jnp.dot(rows_of_slots(first, count), wq_v[...], preferred_element_type=F32)
        store_queries(got, qq, first, count)
        q_along_x(g)

    def far_queries(n):
        got = jnp.dot(rows_of_slots(2 * n, 2), w2_v[...], preferred_element_type=F32)
        store_queries(got, q2, 2 * n, 2)
        send(
            q2.at[pl.ds(2 * n, 2)], qq.at[pl.ds(HALF + 2 * n, 2)], 10, f_rs.at[n], far
        )

    def relay(n):
        landed(qq.at[pl.ds(HALF + 2 * n, 2)], f_rs.at[n])
        q_along_x(4 + n)

    def block_of(slot):
        u = slot % HALF
        sign = turn * (2 * (u % 2) - 1)
        return (z + NZ + HALF * (slot // HALF) + sign * ((u + 1) // 2)) % NZ

    offset = lax.broadcasted_iota(jnp.int32, (BLOCK, HD), 1) - lax.broadcasted_iota(
        jnp.int32, (BLOCK, HD), 0
    )
    row_no = lax.broadcasted_iota(jnp.int32, (16, HD), 0)

    lane = lax.broadcasted_iota(jnp.int32, (1, 2 * NBR), 1)

    def attend(pair, items):
        loaded = []
        for j, slot in items:
            block = block_of(slot)
            rows, bias = [], []
            for k in range(2):
                nbr = ids_s[j, k, block]
                shard = nbr // ROWS
                col = (shard // 2) % NX
                rows.append(
                    ((shard // (2 * NX) * 2 + shard % 2) * 2 + col % 2) * ROWS + nbr % ROWS
                )
                bias.append(jnp.where(col // 2 == x1, 0.0, NEG))
            loaded.append((
                qq[slot, 0] if j == 0 else q_in[j, slot],
                jnp.concatenate([kv[0, rows[0]], kv[0, rows[1]]], axis=0),
                jnp.concatenate([kv[1, rows[0]], kv[1, rows[1]]], axis=0),
                jnp.where(lane < NBR, bias[0], bias[1]),
            ))
        scores = [
            lax.dot_general(q, keys, (((1,), (1,)), ((), ())), preferred_element_type=F32) + bias
            for q, keys, _, bias in loaded
        ]
        expo = [jnp.exp(s) for s in scores]
        denom = [jnp.sum(e, axis=-1, keepdims=True) for e in expo]
        down = [jnp.where(d > 1.0, 0.0625, 1.0) for d in denom]
        inverse = [jnp.where(d > 0.0, 1.0 / (d * w), 0.0) for d, w in zip(denom, down)]
        probs = [(e * w * v).astype(BF) for e, w, v in zip(expo, down, inverse)]
        parts = [
            jnp.dot(p, values, preferred_element_type=F32)
            for p, (_, _, values, _) in zip(probs, loaded)
        ]
        for n in range(0, len(items), 2):
            j = items[n][0]
            total = jnp.zeros((1, HD), F32)
            for a in range(2):
                r_out[j, pair, a * BLOCK : (a + 1) * BLOCK, :] = parts[n + a].astype(BF)
                total += jnp.sum(
                    jnp.where(offset == a * BLOCK, denom[n + a], 0.0), axis=0, keepdims=True
                )
            hi = total.astype(BF).astype(F32)
            mid = (total - hi).astype(BF).astype(F32)
            lo = total - hi - mid
            packed = jnp.where(
                row_no == 0, hi, jnp.where(row_no == 1, mid, jnp.where(row_no == 2, lo, 0.0))
            )
            r_out[j, pair, 2 * BLOCK : RR, :] = packed.astype(BF)

    def serve(pair, slots, parts):
        for g, first, count in parts:
            landed(q_in.at[pl.ds(1, 3), pl.ds(first, count)], q_rs.at[g])
        attend(pair, [(j, slot) for j in (1, 2, 3, 0) for slot in slots])
        for j in (2, 1, 3):
            send(r_out.at[j, pair], r_in.at[j, pair], 11, r_rs.at[pair], x_dev[j])

    ones = jnp.ones((16, HD), BF)

    def sums_of(ref, j, pair):
        return lax.dot_general(
            ref[j, pair, 2 * BLOCK : RR, :], ones, (((0,), (0,)), ((), ())),
            preferred_element_type=F32,
        )

    def out_copy(slot):
        rows = pl.ds(pl.multiple_of(block_of(slot) * BLOCK, BLOCK), BLOCK)
        return pltpu.make_async_copy(out_v.at[slot], out.at[rows], o_sem.at[0])

    def merge(pair, slots):
        landed(r_in.at[pl.ds(1, 3), pair], r_rs.at[pair])
        todo = ((x0, (r_out, 0), (r_in, 2)), (1 - x0, (r_in, 1), (r_in, 3)))
        sums = [[sums_of(ref, j, pair) for ref, j in two] for _, *two in todo]
        vals = [[ref[j, pair, 0 : 2 * BLOCK, :].astype(F32) for ref, j in two] for _, *two in todo]
        for (head, _, _), (la, lb), (va, vb) in zip(todo, sums, vals):
            both = jnp.where(la + lb > 0.0, la + lb, 1.0)
            mixed = ((la / both) * va + (lb / both) * vb).astype(BF)
            columns = pl.ds(pl.multiple_of(head * HD, HD), HD)
            for a, slot in enumerate(slots):
                out_v[slot, :, columns] = mixed[a * BLOCK : (a + 1) * BLOCK]
        for slot in slots:
            out_copy(slot).start()

    loads[0].wait()
    norm()
    pl.semaphore_wait(barrier, len(peers))
    w_far()
    z_first()
    loads[1].wait()
    for j in (1, 2, 3):
        send(ids_v.at[0], ids_v.at[j], 5, i_rs.at[0], x_dev[j])
    loads[2].wait()

    def keys(n, carry):
        part = bank_v.at[pl.ds(n * half, half)]
        pltpu.make_async_copy(part, part, lsem.at[3 + n]).wait()
        project(0, n)
        pass_on(0, n)
        return carry

    lax.fori_loop(0, 2, keys, 0)
    loads[5].wait()

    def values(n, carry):
        project(1, n)
        pass_on(1, n)
        return carry

    lax.fori_loop(0, 2, values, 0)
    loads[6].wait()
    queries(0)
    w_along_y()
    y_step(1, 0)
    neighbour(0)
    y_step(1, 1)
    neighbour(1)
    landed(ids_v.at[pl.ds(1, 3)], i_rs.at[0])
    to_smem = pltpu.make_async_copy(ids_v, ids_s, lsem.at[7])
    to_smem.start()
    z_step(1, 0)
    w_along_x()
    y_step(2, 0)
    z_step(1, 1)
    queries(1)
    y_step(1, 2)
    z_step(2, 0)
    y_step(2, 1)
    w_on()
    y_step(1, 3)
    w_last()
    z_step(2, 1)
    y_step(3, 0)
    queries(2)
    w_whole()
    far_queries(0)
    far_queries(1)
    y_step(2, 2)
    z_step(3, 0)
    y_step(3, 1)
    z_step(3, 1)
    y_step(2, 3)
    queries(3)
    far_queries(2)
    y_step(3, 2, ways=(1,))
    y_step(4, 0)
    y_step(3, 2, ways=(0,))
    y_step(3, 3, ways=(1,))
    relay(0)
    y_step(4, 1)
    y_step(4, 2)
    relay(1)
    y_step(3, 3, ways=(0,))
    y_step(4, 3)
    relay(2)
    to_smem.wait()
    landed(kv.at[0], b_rs.at[0])
    serve(0, (0, 5), [(0, 0, 1), (3, 5, 1)])

    def serve_near(n, carry):
        serve(1 + n, (1 + 2 * n, 2 + 2 * n), [(1 + n, 1 + 2 * n, 2)])
        return carry

    def serve_away(n, carry):
        first = HALF + 2 * n
        serve(3 + n, (first, first + 1), [(4 + n, first, 2)])
        return carry

    lax.fori_loop(0, 2, serve_near, 0)
    lax.fori_loop(0, 3, serve_away, 0)
    merge(0, (0, 5))

    def merge_near(n, carry):
        merge(1 + n, (1 + 2 * n, 2 + 2 * n))
        return carry

    def merge_away(n, carry):
        merge(3 + n, (HALF + 2 * n, HALF + 1 + 2 * n))
        return carry

    lax.fori_loop(0, 2, merge_near, 0)
    lax.fori_loop(0, 3, merge_away, 0)

    for family, like in enumerate((
        w2_v.at[pl.ds(0, 128)],
        w2_v.at[pl.ds(0, 3 * 128)],
        w2_v.at[pl.ds(0, 1536)],
        w2_v.at[pl.ds(0, D // 2)],
        zb.at[pl.ds(0, 5)],
        ids_v.at[pl.ds(1, 3)],
        kv.at[0, pl.ds(0, 112)],
        kv.at[0],
        kvs,
        q_in.at[pl.ds(1, 3)],
        q2,
        r_in.at[pl.ds(1, 3)],
    )):
        all_sent(like, family)
    pltpu.make_async_copy(out_v, out_v, o_sem.at[0]).wait()


def per_device(hidden, norm_gain, query_weight, key_weight, value_weight, bank, neighbour_ids):
    hbm = pl.BlockSpec(memory_space=pl.ANY)
    vmem = pl.BlockSpec(memory_space=pltpu.VMEM)
    dma = pltpu.SemaphoreType.DMA
    width = query_weight.shape[1]
    return pl.pallas_call(
        kernel,
        out_shape=jax.ShapeDtypeStruct((NZ * BLOCK, width), BF),
        in_specs=[hbm, vmem, hbm, hbm, hbm, hbm, hbm],
        out_specs=hbm,
        scratch_shapes=[
            pltpu.VMEM((BLOCK, D), BF),
            pltpu.VMEM((D, width), BF),
            pltpu.VMEM((D, width), BF),
            pltpu.VMEM((D, width), BF),
            pltpu.VMEM((D, width), BF),
            pltpu.VMEM((ROWS, NBR, D), BF),
            pltpu.VMEM((HALF, BLOCK, D), BF),
            pltpu.VMEM((2, NY * 2 * 2 * ROWS, NBR, HD), BF),
            pltpu.VMEM((2, ROWS, NBR, HD), BF),
            pltpu.VMEM((NZ, 2, BLOCK, HD), BF),
            pltpu.VMEM((HALF, 2, BLOCK, HD), BF),
            pltpu.VMEM((NX, NZ, BLOCK, HD), BF),
            pltpu.VMEM((NX, HALF, RR, HD), BF),
            pltpu.VMEM((NX, HALF, RR, HD), BF),
            pltpu.VMEM((NX, 2, NZ), jnp.int32),
            pltpu.SMEM((NX, 2, NZ), jnp.int32),
            dma((8,)),
            dma((12,)),
            dma((2, 3, 2)),
            dma((2, 4, 4)),
            dma((2,)),
            dma((1,)),
            dma((7,)),
            dma((6,)),
            dma((1,)),
            dma((1,)),
            dma((1,)),
            dma((2, 2)),
            dma((1,)),
            dma((3,)),
            pltpu.VMEM((NZ, BLOCK, width), BF),
            dma((1,)),
        ],
        compiler_params=pltpu.CompilerParams(
            collective_id=0, has_side_effects=True, vmem_limit_bytes=56 * 1024 * 1024
        ),
    )(
        hidden, norm_gain.reshape(1, D), query_weight, key_weight, value_weight, bank, neighbour_ids.T
    )


def solution(mesh):
    placed = (
        P(("db", "mp"), None),
        P(),
        P(None, "mp"),
        P(None, "mp"),
        P(None, "mp"),
        P("db", None, None),
        P("db", None),
    )
    return jax.shard_map(
        per_device, mesh=mesh, in_specs=placed, out_specs=P("db", "mp"), check_vma=False
    )
```

```python
import jax
import jax.numpy as jnp
from jax import lax
from jax.experimental import pallas as pl
from jax.experimental.pallas import tpu as pltpu
from jax.sharding import PartitionSpec as P

HD = 128
BLOCK = 64
NBR = 128
EPS = 1e-6
NX, NY, NZ = 4, 8, 12
D = 4096
ROWS = 4
NEG = -1e30
MESH = pl.DeviceIdType.MESH
BF = jnp.bfloat16
F32 = jnp.float32


GROUPS = ((0, 1), (1, 2), (3, 2), (5, 1), (6, 2), (8, 2), (10, 2))
HALF = NZ // 2


def kernel(
    hidden, gain, wq, wk, wv, bank, ids, out,
    hid_v, wq_v, w2_v, wk_v, wv_v, bank_v, zb, kv, kvs, qq, q2, q_in, r_out, r_in, ids_v, ids_s,
    lsem, s_sem, z_rs, y_rs, x_rs, b_rs, q_rs, r_rs, i_rs, w0_rs, wy_rs, wx_rs, wb_rs, f_rs,
    gain_v, l_out, l_in, l_rs,
):
    db = lax.axis_index("db")
    z = lax.axis_index("mp")
    c = db % 2
    x = (db // 2) % NX
    y = db // (2 * NX)
    x0 = x % 2
    x1 = x // 2
    turn = 1 - 2 * c

    def dev(yy, xx, cc, zz):
        return {"db": (yy * NX + xx) * 2 + cc, "mp": zz}

    xs = (x, x + 1 - 2 * x0, (x + 2) % NX, NX - 1 - x)
    z_dev = (dev(y, x, c, (z + NZ - turn) % NZ), dev(y, x, c, (z + NZ + turn) % NZ))
    far = dev(y, x, c, (z + HALF) % NZ)
    y_dev = (dev((y + 1) % NY, x, c, z), dev((y + NY - 1) % NY, x, c, z))
    away = 2 * (y % 2) - 1
    y_three = tuple(dev((y + NY + away * d) % NY, x, c, z) for d in (1, 2, 3))
    x_dev = tuple(dev(y, xx, c, z) for xx in xs)
    ring = (dev(y, (x + 1) % NX, c, z), dev(y, (x + NX - 1) % NX, c, z))
    sib = dev(y, x, 1 - c, z)
    peers = z_dev + (far,) + tuple(dev((y + d) % NY, x, c, z) for d in (1, 2, 3, 5, 6, 7)) + x_dev[1:] + (sib,)

    half = ROWS // 2
    loads = [
        pltpu.make_async_copy(a, b, lsem.at[n])
        for n, (a, b) in enumerate((
            (hidden, hid_v),
            (gain, gain_v),
            (ids, ids_v.at[0]),
            (wk, wk_v),
            (bank.at[pl.ds(0, half)], bank_v.at[pl.ds(0, half)]),
            (bank.at[pl.ds(half, half)], bank_v.at[pl.ds(half, half)]),
            (wv, wv_v),
            (wq, wq_v),
        ))
    ]
    for load in loads:
        load.start()
    barrier = pltpu.get_barrier_semaphore()
    for peer in peers:
        pl.semaphore_signal(barrier, inc=1, device_id=peer, device_id_type=MESH)

    def copy(src, dst, ss, rs, to):
        return pltpu.make_async_remote_copy(
            src_ref=src, dst_ref=dst, send_sem=ss, recv_sem=rs, device_id=to, device_id_type=MESH
        )

    def send(src, dst, family, rs, to):
        copy(src, dst, s_sem.at[family], rs, to).start()

    def landed(dst, rs):
        copy(dst, dst, s_sem.at[0], rs, sib).wait_recv()

    def all_sent(like, family):
        copy(like, like, s_sem.at[family], s_sem.at[family], sib).wait_send()

    def norm():
        def norm_rows(n, carry):
            rows = pl.ds(pl.multiple_of(n * 16, 16), 16)
            stream = hid_v[rows, :].astype(F32)
            factor = lax.rsqrt(jnp.mean(stream * stream, axis=-1, keepdims=True) + EPS)
            zb[0, rows, :] = (stream * factor * gain_v[...]).astype(BF)
            return carry

        lax.fori_loop(0, BLOCK // 16, norm_rows, 0)

    def w_rows(first, count):
        return w2_v.at[pl.ds(pl.multiple_of(first, 64), count)]

    def w_slice(yy):
        return w_rows(x * 1024 + c * 512 + yy // 2 * 128, 128)

    def w_far():
        first = pl.multiple_of(x * 1024 + c * 512 + y // 2 * 128, 128)
        send(wq.at[pl.ds(first, 128)], w_slice(y), 0, w0_rs.at[0], far)

    def w_along_y():
        landed(w_slice(y), w0_rs.at[0])
        for to in y_three:
            send(w_slice(y), w_slice(y), 1, wy_rs.at[0], to)

    def w_block(xx, cc):
        return w_rows(xx * 1024 + cc * 512, 512)

    def w_half(xx, cc, half):
        return w_rows(xx * 1024 + cc * 512 + half * 256, 256)

    def w_along_x():
        landed(w2_v.at[pl.ds(0, 3 * 128)], wy_rs.at[0])
        own_block = w_block(x, c)
        for way in range(2):
            send(own_block, own_block, 2, wx_rs.at[way, 0], ring[way])
        send(own_block, own_block, 3, wb_rs.at[0], sib)

    def w_from(way):
        return (x + NX - 1) % NX if way == 0 else (x + 1) % NX

    def w_on():
        for way in range(2):
            block = w_block(w_from(way), c)
            landed(block, wx_rs.at[way, 0])
            half = w_half(w_from(way), c, way)
            send(half, half, 2, wx_rs.at[way, 1], ring[way])
            send(block, block, 3, wb_rs.at[0], sib)

    def w_last():
        for way in range(2):
            half = w_half((x + 2) % NX, c, way)
            landed(half, wx_rs.at[way, 1])
            send(half, half, 3, wb_rs.at[0], sib)

    def w_whole():
        landed(w2_v.at[pl.ds(0, D // 2)], wb_rs.at[0])

    STEPS = (3, 2)

    def z_part(slot, sub):
        return zb.at[slot, pl.ds(sub * 32, 32), :]

    def z_slot(way, s):
        return 0 if s == 0 else 2 * s - 1 + way

    def z_send(way, s, sub):
        send(
            z_part(z_slot(way, s), sub), z_part(z_slot(way, s + 1), sub),
            4, z_rs.at[way, s, sub], z_dev[way],
        )

    def z_step(s, sub):
        for way in range(2):
            if s <= STEPS[way]:
                landed(z_part(z_slot(way, s), sub), z_rs.at[way, s - 1, sub])
                if s < STEPS[way]:
                    z_send(way, s, sub)

    def z_first():
        for sub in range(2):
            for way in range(2):
                z_send(way, 0, sub)

    def unit(yy, cc, bit):
        return ((yy * 2 + cc) * 2 + bit) * ROWS

    own = unit(y, c, x0)

    def project(which, n):
        got = jnp.dot(
            bank_v[pl.ds(n * half, half)].reshape(half * NBR, D), (wk_v, wv_v)[which][...],
            preferred_element_type=F32,
        )
        low, high = got[:, :HD], got[:, HD:]
        mine = jnp.where(x0 == 0, low, high).astype(BF)
        other = jnp.where(x0 == 0, high, low).astype(BF)
        for a in range(half):
            kv[which, own + n * half + a] = mine[a * NBR : (a + 1) * NBR]
            kvs[which, n * half + a] = other[a * NBR : (a + 1) * NBR]

    def pass_on(which, n):
        part = kv.at[which, pl.ds(own + n * half, half)]
        for way in range(2):
            send(part, part, 6, y_rs.at[way, 0, which], y_dev[way])
        send(kvs.at[which, pl.ds(n * half, half)], part, 8, x_rs.at[which], x_dev[1])
        send(part, part, 7, b_rs.at[0], sib)

    def y_at(way, s):
        return (y + NY - s) % NY if way == 0 else (y + s) % NY

    def kv_part(yy, cc, sub):
        return kv.at[sub % 2, pl.ds(unit(yy, cc, x0 if sub < 2 else 1 - x0), ROWS)]

    def y_send(way, s, sub):
        part = kv_part(y_at(way, s), c, sub)
        send(part, part, 6, y_rs.at[way, s, sub], y_dev[way])

    def b_send(way, s, sub):
        part = kv_part(y_at(way, s), c, sub)
        send(part, part, 7, b_rs.at[0], sib)

    def y_needed(way, s, sub):
        return s < 4 or sub // 2 == way

    def y_first(sub):
        for way in range(2):
            y_send(way, 0, sub)
        b_send(0, 0, sub)

    def y_step(s, *subs, ways=(0, 1)):
        for sub in subs:
            for way in ways:
                if y_needed(way, s, sub):
                    part = kv_part(y_at(way, s), c, sub)
                    landed(part, y_rs.at[way, s - 1, sub])
                    if s < 4 and y_needed(way, s + 1, sub):
                        y_send(way, s, sub)
                    b_send(way, s, sub)

    def neighbour(which):
        landed(kv_part(y, c, 2 + which), x_rs.at[which])
        y_first(2 + which)

    scale = HD ** (-0.5)

    def store_queries(got, ref, first, count):
        got = got * scale
        low, high = got[:, :HD], got[:, HD:]
        mine = jnp.where(x0 == 0, low, high).astype(BF)
        other = jnp.where(x0 == 0, high, low).astype(BF)
        for a in range(count):
            ref[first + a, 0] = mine[a * BLOCK : (a + 1) * BLOCK]
            ref[first + a, 1] = other[a * BLOCK : (a + 1) * BLOCK]

    def rows_of_slots(first, count):
        return zb[first : first + count].reshape(count * BLOCK, D)

    def q_along_x(g):
        first, count = GROUPS[g]
        for j in (2, 1, 3):
            send(
                qq.at[pl.ds(first, count), 0 if j == 2 else 1], q_in.at[j, pl.ds(first, count)],
                9, q_rs.at[g], x_dev[j],
            )

    def queries(g):
        first, count = GROUPS[g]
        got = jnp.dot(rows_of_slots(first, count), wq_v[...], preferred_element_type=F32)
        store_queries(got, qq, first, count)
        q_along_x(g)

    def far_queries(n):
        got = jnp.dot(rows_of_slots(2 * n, 2), w2_v[...], preferred_element_type=F32)
        store_queries(got, q2, 2 * n, 2)
        send(
            q2.at[pl.ds(2 * n, 2)], qq.at[pl.ds(HALF + 2 * n, 2)], 10, f_rs.at[n], far
        )

    def relay(n):
        landed(qq.at[pl.ds(HALF + 2 * n, 2)], f_rs.at[n])
        q_along_x(4 + n)

    def block_of(slot):
        u = slot % HALF
        sign = turn * (2 * (u % 2) - 1)
        return (z + NZ + HALF * (slot // HALF) + sign * ((u + 1) // 2)) % NZ

    offset = lax.broadcasted_iota(jnp.int32, (BLOCK, HD), 1) - lax.broadcasted_iota(
        jnp.int32, (BLOCK, HD), 0
    )
    row_no = lax.broadcasted_iota(jnp.int32, (16, HD), 0)

    lane = lax.broadcasted_iota(jnp.int32, (1, 2 * NBR), 1)

    def attend(pair, items):
        loaded = []
        for j, slot in items:
            block = block_of(slot)
            rows, bias = [], []
            for k in range(2):
                nbr = ids_s[j, k, block]
                shard = nbr // ROWS
                col = (shard // 2) % NX
                rows.append(
                    ((shard // (2 * NX) * 2 + shard % 2) * 2 + col % 2) * ROWS + nbr % ROWS
                )
                bias.append(jnp.where(col // 2 == x1, 0.0, NEG))
            loaded.append((
                qq[slot, 0] if j == 0 else q_in[j, slot],
                jnp.concatenate([kv[0, rows[0]], kv[0, rows[1]]], axis=0),
                jnp.concatenate([kv[1, rows[0]], kv[1, rows[1]]], axis=0),
                jnp.where(lane < NBR, bias[0], bias[1]),
            ))
        scores = [
            lax.dot_general(q, keys, (((1,), (1,)), ((), ())), preferred_element_type=F32) + bias
            for q, keys, _, bias in loaded
        ]
        expo = [jnp.exp(s) for s in scores]
        denom = [jnp.sum(e, axis=-1, keepdims=True) for e in expo]
        down = [jnp.where(d > 1.0, 0.0625, 1.0) for d in denom]
        inverse = [jnp.where(d > 0.0, 1.0 / (d * w), 0.0) for d, w in zip(denom, down)]
        probs = [(e * w * v).astype(BF) for e, w, v in zip(expo, down, inverse)]
        parts = [
            jnp.dot(p, values, preferred_element_type=F32)
            for p, (_, _, values, _) in zip(probs, loaded)
        ]
        for n in range(0, len(items), 2):
            j = items[n][0]
            total = jnp.zeros((1, HD), F32)
            for a in range(2):
                r_out[j, pair, a * BLOCK : (a + 1) * BLOCK, :] = parts[n + a].astype(BF)
                total += jnp.sum(
                    jnp.where(offset == a * BLOCK, denom[n + a], 0.0), axis=0, keepdims=True
                )
            l_out[j, pair // 3, pl.ds(pair % 3, 1), :] = total

    def serve(pair, slots, parts):
        for g, first, count in parts:
            landed(q_in.at[pl.ds(1, 3), pl.ds(first, count)], q_rs.at[g])
        attend(pair, [(j, slot) for j in (1, 2, 3, 0) for slot in slots])
        for j in (2, 1, 3):
            send(r_out.at[j, pair], r_in.at[j, pair], 11, r_rs.at[pair], x_dev[j])

    ones = jnp.ones((16, HD), BF)

    def send_sums(third):
        for j in (2, 1, 3):
            send(l_out.at[j, third], l_in.at[j, third], 12, l_rs.at[third], x_dev[j])

    def column(row):
        hi = row.astype(BF).astype(F32)
        mid = (row - hi).astype(BF).astype(F32)
        lo = row - hi - mid
        terms = jnp.where(
            row_no == 0, hi, jnp.where(row_no == 1, mid, jnp.where(row_no == 2, lo, 0.0))
        )
        return lax.dot_general(
            terms.astype(BF), ones, (((0,), (0,)), ((), ())), preferred_element_type=F32
        )

    def merge(pair, slots):
        landed(r_in.at[pl.ds(1, 3), pair], r_rs.at[pair])
        todo = (
            (x0, (r_out, l_out, 0), (r_in, l_in, 2)),
            (1 - x0, (r_in, l_in, 1), (r_in, l_in, 3)),
        )
        weights, vals = [], []
        for _, *two in todo:
            la, lb = (sums[j, pair // 3, pl.ds(pair % 3, 1), :] for _, sums, j in two)
            weights.append(column(la / jnp.where(la + lb > 0.0, la + lb, 1.0)))
            vals.append([ref[j, pair].astype(F32) for ref, _, j in two])
        for (head, _, _), wa, (va, vb) in zip(todo, weights, vals):
            mixed = (wa * va + (1.0 - wa) * vb).astype(BF)
            columns = pl.ds(pl.multiple_of(head * HD, HD), HD)
            for a, slot in enumerate(slots):
                rows = pl.ds(pl.multiple_of(block_of(slot) * BLOCK, BLOCK), BLOCK)
                out[rows, columns] = mixed[a * BLOCK : (a + 1) * BLOCK]

    loads[0].wait()
    loads[1].wait()
    norm()
    pl.semaphore_wait(barrier, len(peers))
    w_far()
    z_first()
    loads[2].wait()
    for j in (1, 2, 3):
        send(ids_v.at[0], ids_v.at[j], 5, i_rs.at[0], x_dev[j])
    loads[3].wait()

    def keys(n, carry):
        part = bank_v.at[pl.ds(n * half, half)]
        pltpu.make_async_copy(part, part, lsem.at[4 + n]).wait()
        project(0, n)
        pass_on(0, n)
        return carry

    lax.fori_loop(0, 2, keys, 0)
    loads[6].wait()

    def values(n, carry):
        project(1, n)
        pass_on(1, n)
        return carry

    lax.fori_loop(0, 2, values, 0)
    loads[7].wait()
    queries(0)
    w_along_y()
    y_step(1, 0)
    neighbour(0)
    y_step(1, 1)
    neighbour(1)
    landed(ids_v.at[pl.ds(1, 3)], i_rs.at[0])
    to_smem = pltpu.make_async_copy(ids_v, ids_s, lsem.at[8])
    to_smem.start()
    z_step(1, 0)
    w_along_x()
    y_step(2, 0)
    z_step(1, 1)
    queries(1)
    y_step(1, 2)
    z_step(2, 0)
    y_step(2, 1)
    w_on()
    y_step(1, 3)
    w_last()
    z_step(2, 1)
    y_step(3, 0)
    queries(2)
    w_whole()
    far_queries(0)
    far_queries(1)
    y_step(2, 2)
    z_step(3, 0)
    y_step(3, 1)
    z_step(3, 1)
    y_step(2, 3)
    queries(3)
    far_queries(2)
    y_step(3, 2, ways=(1,))
    y_step(4, 0)
    y_step(3, 2, ways=(0,))
    y_step(3, 3, ways=(1,))
    relay(0)
    y_step(4, 1)
    y_step(4, 2)
    relay(1)
    y_step(3, 3, ways=(0,))
    y_step(4, 3)
    relay(2)
    to_smem.wait()
    landed(kv.at[0], b_rs.at[0])
    serve(0, (0, 5), [(0, 0, 1), (3, 5, 1)])

    def serve_near(n, carry):
        serve(1 + n, (1 + 2 * n, 2 + 2 * n), [(1 + n, 1 + 2 * n, 2)])
        return carry

    def serve_away(n, carry):
        first = HALF + 2 * n
        serve(3 + n, (first, first + 1), [(4 + n, first, 2)])
        return carry

    lax.fori_loop(0, 2, serve_near, 0)
    send_sums(0)
    lax.fori_loop(0, 3, serve_away, 0)
    send_sums(1)
    landed(l_in.at[pl.ds(1, 3), 0], l_rs.at[0])
    merge(0, (0, 5))

    def merge_near(n, carry):
        merge(1 + n, (1 + 2 * n, 2 + 2 * n))
        return carry

    def merge_away(n, carry):
        merge(3 + n, (HALF + 2 * n, HALF + 1 + 2 * n))
        return carry

    lax.fori_loop(0, 2, merge_near, 0)
    landed(l_in.at[pl.ds(1, 3), 1], l_rs.at[1])
    lax.fori_loop(0, 3, merge_away, 0)

    for family, like in enumerate((
        w2_v.at[pl.ds(0, 128)],
        w2_v.at[pl.ds(0, 3 * 128)],
        w2_v.at[pl.ds(0, 1536)],
        w2_v.at[pl.ds(0, D // 2)],
        zb.at[pl.ds(0, 5)],
        ids_v.at[pl.ds(1, 3)],
        kv.at[0, pl.ds(0, 112)],
        kv.at[0],
        kvs,
        q_in.at[pl.ds(1, 3)],
        q2,
        r_in.at[pl.ds(1, 3)],
        l_in.at[pl.ds(1, 3)],
    )):
        all_sent(like, family)


def per_device(hidden, norm_gain, query_weight, key_weight, value_weight, bank, neighbour_ids):
    hbm = pl.BlockSpec(memory_space=pl.ANY)
    dma = pltpu.SemaphoreType.DMA
    width = query_weight.shape[1]
    return pl.pallas_call(
        kernel,
        out_shape=pltpu.VMEM((NZ * BLOCK, width), BF),
        in_specs=[hbm] * 7,
        out_specs=pl.BlockSpec(memory_space=pltpu.VMEM),
        scratch_shapes=[
            pltpu.VMEM((BLOCK, D), BF),
            pltpu.VMEM((D, width), BF),
            pltpu.VMEM((D, width), BF),
            pltpu.VMEM((D, width), BF),
            pltpu.VMEM((D, width), BF),
            pltpu.VMEM((ROWS, NBR, D), BF),
            pltpu.VMEM((HALF, BLOCK, D), BF),
            pltpu.VMEM((2, NY * 2 * 2 * ROWS, NBR, HD), BF),
            pltpu.VMEM((2, ROWS, NBR, HD), BF),
            pltpu.VMEM((NZ, 2, BLOCK, HD), BF),
            pltpu.VMEM((HALF, 2, BLOCK, HD), BF),
            pltpu.VMEM((NX, NZ, BLOCK, HD), BF),
            pltpu.VMEM((NX, HALF, 2 * BLOCK, HD), BF),
            pltpu.VMEM((NX, HALF, 2 * BLOCK, HD), BF),
            pltpu.VMEM((NX, 2, NZ), jnp.int32),
            pltpu.SMEM((NX, 2, NZ), jnp.int32),
            dma((9,)),
            dma((13,)),
            dma((2, 3, 2)),
            dma((2, 4, 4)),
            dma((2,)),
            dma((1,)),
            dma((7,)),
            dma((6,)),
            dma((1,)),
            dma((1,)),
            dma((1,)),
            dma((2, 2)),
            dma((1,)),
            dma((3,)),
            pltpu.VMEM((1, D), F32),
            pltpu.VMEM((NX, 2, 8, HD), F32),
            pltpu.VMEM((NX, 2, 8, HD), F32),
            dma((2,)),
        ],
        compiler_params=pltpu.CompilerParams(
            collective_id=0, has_side_effects=True, vmem_limit_bytes=56 * 1024 * 1024
        ),
    )(
        hidden, norm_gain.reshape(1, D), query_weight, key_weight, value_weight, bank, neighbour_ids.T
    )


def solution(mesh):
    placed = (
        P(("db", "mp"), None),
        P(),
        P(None, "mp"),
        P(None, "mp"),
        P(None, "mp"),
        P("db", None, None),
        P("db", None),
    )
    return jax.shard_map(
        per_device, mesh=mesh, in_specs=placed, out_specs=P("db", "mp"), check_vma=False
    )
```

```python
import jax
import jax.numpy as jnp
from jax import lax
from jax.experimental import pallas as pl
from jax.experimental.pallas import tpu as pltpu
from jax.sharding import PartitionSpec as P

HD = 128
BLOCK = 64
NBR = 128
EPS = 1e-6
NX, NY, NZ = 4, 8, 12
D = 4096
ROWS = 4
NEG = -1e30
MESH = pl.DeviceIdType.MESH
BF = jnp.bfloat16
F32 = jnp.float32


GROUPS = ((0, 1), (1, 2), (3, 2), (5, 1), (6, 2), (8, 2), (10, 2))
HALF = NZ // 2


def kernel(
    hidden, gain, wq, wk, wv, bank, ids, out,
    hid_v, wq_v, w2_v, wk_v, wv_v, bank_v, zb, kv, kvs, qq, q2, q_in, r_out, r_in, ids_v, ids_s,
    lsem, s_sem, z_rs, y_rs, x_rs, b_rs, q_rs, r_rs, i_rs, w0_rs, wy_rs, wx_rs, wb_rs, f_rs,
    gain_v, l_out, l_in, l_rs,
):
    db = lax.axis_index("db")
    z = lax.axis_index("mp")
    c = db % 2
    x = (db // 2) % NX
    y = db // (2 * NX)
    x0 = x % 2
    x1 = x // 2
    turn = 1 - 2 * c

    def dev(yy, xx, cc, zz):
        return {"db": (yy * NX + xx) * 2 + cc, "mp": zz}

    xs = (x, x + 1 - 2 * x0, (x + 2) % NX, NX - 1 - x)
    z_dev = (dev(y, x, c, (z + NZ - turn) % NZ), dev(y, x, c, (z + NZ + turn) % NZ))
    far = dev(y, x, c, (z + HALF) % NZ)
    y_dev = (dev((y + 1) % NY, x, c, z), dev((y + NY - 1) % NY, x, c, z))
    y_others = tuple(dev((y + d) % NY, x, c, z) for d in (1, 7, 2, 6, 3, 5, 4))
    x_dev = tuple(dev(y, xx, c, z) for xx in xs)
    ring = (dev(y, (x + 1) % NX, c, z), dev(y, (x + NX - 1) % NX, c, z))
    sib = dev(y, x, 1 - c, z)
    peers = z_dev + (far,) + y_others + x_dev[1:] + (sib,)

    half = ROWS // 2
    loads = [
        pltpu.make_async_copy(a, b, lsem.at[n])
        for n, (a, b) in enumerate((
            (hidden, hid_v),
            (gain, gain_v),
            (ids, ids_v.at[0]),
            (wk, wk_v),
            (bank.at[pl.ds(0, half)], bank_v.at[pl.ds(0, half)]),
            (bank.at[pl.ds(half, half)], bank_v.at[pl.ds(half, half)]),
            (wv, wv_v),
            (wq, wq_v),
        ))
    ]
    for load in loads:
        load.start()
    barrier = pltpu.get_barrier_semaphore()
    for peer in peers:
        pl.semaphore_signal(barrier, inc=1, device_id=peer, device_id_type=MESH)

    def copy(src, dst, ss, rs, to):
        return pltpu.make_async_remote_copy(
            src_ref=src, dst_ref=dst, send_sem=ss, recv_sem=rs, device_id=to, device_id_type=MESH
        )

    def send(src, dst, family, rs, to):
        copy(src, dst, s_sem.at[family], rs, to).start()

    def landed(dst, rs):
        copy(dst, dst, s_sem.at[0], rs, sib).wait_recv()

    def all_sent(like, family):
        copy(like, like, s_sem.at[family], s_sem.at[family], sib).wait_send()

    def norm():
        def norm_rows(n, carry):
            rows = pl.ds(pl.multiple_of(n * 16, 16), 16)
            stream = hid_v[rows, :].astype(F32)
            factor = lax.rsqrt(jnp.mean(stream * stream, axis=-1, keepdims=True) + EPS)
            zb[0, rows, :] = (stream * factor * gain_v[...]).astype(BF)
            return carry

        lax.fori_loop(0, BLOCK // 16, norm_rows, 0)

    def w_rows(first, count):
        return w2_v.at[pl.ds(pl.multiple_of(first, 64), count)]

    def w_slice(yy):
        return w_rows(x * 1024 + c * 512 + yy * 64, 64)

    def w_far():
        first = pl.multiple_of(x * 1024 + c * 512 + y * 64, 64)
        send(wq.at[pl.ds(first, 64)], w_slice(y), 0, w0_rs.at[0], far)

    def w_along_y():
        landed(w_slice(y), w0_rs.at[0])
        for to in y_others:
            send(w_slice(y), w_slice(y), 1, wy_rs.at[0], to)

    def w_block(xx, cc):
        return w_rows(xx * 1024 + cc * 512, 512)

    def w_half(xx, cc, half):
        return w_rows(xx * 1024 + cc * 512 + half * 256, 256)

    def w_along_x():
        landed(w2_v.at[pl.ds(0, 7 * 64)], wy_rs.at[0])
        own_block = w_block(x, c)
        for way in range(2):
            send(own_block, own_block, 2, wx_rs.at[way, 0], ring[way])
        send(own_block, own_block, 3, wb_rs.at[0], sib)

    def w_from(way):
        return (x + NX - 1) % NX if way == 0 else (x + 1) % NX

    def w_on():
        for way in range(2):
            block = w_block(w_from(way), c)
            landed(block, wx_rs.at[way, 0])
            half = w_half(w_from(way), c, way)
            send(half, half, 2, wx_rs.at[way, 1], ring[way])
            send(block, block, 3, wb_rs.at[0], sib)

    def w_last():
        for way in range(2):
            half = w_half((x + 2) % NX, c, way)
            landed(half, wx_rs.at[way, 1])
            send(half, half, 3, wb_rs.at[0], sib)

    def w_whole():
        landed(w2_v.at[pl.ds(0, D // 2)], wb_rs.at[0])

    STEPS = (3, 2)

    def z_part(slot, sub):
        return zb.at[slot, pl.ds(sub * 32, 32), :]

    def z_slot(way, s):
        return 0 if s == 0 else 2 * s - 1 + way

    def z_send(way, s, sub):
        send(
            z_part(z_slot(way, s), sub), z_part(z_slot(way, s + 1), sub),
            4, z_rs.at[way, s, sub], z_dev[way],
        )

    def z_step(s, sub):
        for way in range(2):
            if s <= STEPS[way]:
                landed(z_part(z_slot(way, s), sub), z_rs.at[way, s - 1, sub])
                if s < STEPS[way]:
                    z_send(way, s, sub)

    def z_first():
        for sub in range(2):
            for way in range(2):
                z_send(way, 0, sub)

    def unit(yy, cc, bit):
        return ((yy * 2 + cc) * 2 + bit) * ROWS

    own = unit(y, c, x0)

    def project(which, n):
        got = jnp.dot(
            bank_v[pl.ds(n * half, half)].reshape(half * NBR, D), (wk_v, wv_v)[which][...],
            preferred_element_type=F32,
        )
        low, high = got[:, :HD], got[:, HD:]
        mine = jnp.where(x0 == 0, low, high).astype(BF)
        other = jnp.where(x0 == 0, high, low).astype(BF)
        for a in range(half):
            kv[which, own + n * half + a] = mine[a * NBR : (a + 1) * NBR]
            kvs[which, n * half + a] = other[a * NBR : (a + 1) * NBR]

    def pass_on(which, n):
        part = kv.at[which, pl.ds(own + n * half, half)]
        for way in range(2):
            send(part, part, 6, y_rs.at[way, 0, which], y_dev[way])
        send(kvs.at[which, pl.ds(n * half, half)], part, 8, x_rs.at[which], x_dev[1])
        send(part, part, 7, b_rs.at[0], sib)

    def y_at(way, s):
        return (y + NY - s) % NY if way == 0 else (y + s) % NY

    def kv_part(yy, cc, sub):
        return kv.at[sub % 2, pl.ds(unit(yy, cc, x0 if sub < 2 else 1 - x0), ROWS)]

    def y_send(way, s, sub):
        part = kv_part(y_at(way, s), c, sub)
        send(part, part, 6, y_rs.at[way, s, sub], y_dev[way])

    def b_send(way, s, sub):
        part = kv_part(y_at(way, s), c, sub)
        send(part, part, 7, b_rs.at[0], sib)

    def y_needed(way, s, sub):
        return s < 4 or sub // 2 == way

    def y_first(sub):
        for way in range(2):
            y_send(way, 0, sub)
        b_send(0, 0, sub)

    def y_step(s, *subs, ways=(0, 1)):
        for sub in subs:
            for way in ways:
                if y_needed(way, s, sub):
                    part = kv_part(y_at(way, s), c, sub)
                    landed(part, y_rs.at[way, s - 1, sub])
                    if s < 4 and y_needed(way, s + 1, sub):
                        y_send(way, s, sub)
                    b_send(way, s, sub)

    def neighbour(which):
        landed(kv_part(y, c, 2 + which), x_rs.at[which])
        y_first(2 + which)

    scale = HD ** (-0.5)

    def store_queries(got, ref, first, count):
        got = got * scale
        low, high = got[:, :HD], got[:, HD:]
        mine = jnp.where(x0 == 0, low, high).astype(BF)
        other = jnp.where(x0 == 0, high, low).astype(BF)
        for a in range(count):
            ref[first + a, 0] = mine[a * BLOCK : (a + 1) * BLOCK]
            ref[first + a, 1] = other[a * BLOCK : (a + 1) * BLOCK]

    def rows_of_slots(first, count):
        return zb[first : first + count].reshape(count * BLOCK, D)

    def q_along_x(g):
        first, count = GROUPS[g]
        for j in (2, 1, 3):
            send(
                qq.at[pl.ds(first, count), 0 if j == 2 else 1], q_in.at[j, pl.ds(first, count)],
                9, q_rs.at[g], x_dev[j],
            )

    def queries(g):
        first, count = GROUPS[g]
        got = jnp.dot(rows_of_slots(first, count), wq_v[...], preferred_element_type=F32)
        store_queries(got, qq, first, count)
        q_along_x(g)

    def far_queries(n):
        got = jnp.dot(rows_of_slots(2 * n, 2), w2_v[...], preferred_element_type=F32)
        store_queries(got, q2, 2 * n, 2)
        send(
            q2.at[pl.ds(2 * n, 2)], qq.at[pl.ds(HALF + 2 * n, 2)], 10, f_rs.at[n], far
        )

    def relay(n):
        landed(qq.at[pl.ds(HALF + 2 * n, 2)], f_rs.at[n])
        q_along_x(4 + n)

    def block_of(slot):
        u = slot % HALF
        sign = turn * (2 * (u % 2) - 1)
        return (z + NZ + HALF * (slot // HALF) + sign * ((u + 1) // 2)) % NZ

    offset = lax.broadcasted_iota(jnp.int32, (BLOCK, HD), 1) - lax.broadcasted_iota(
        jnp.int32, (BLOCK, HD), 0
    )
    row_no = lax.broadcasted_iota(jnp.int32, (16, HD), 0)

    lane = lax.broadcasted_iota(jnp.int32, (1, 2 * NBR), 1)

    def attend(pair, items):
        loaded = []
        for j, slot in items:
            block = block_of(slot)
            rows, bias = [], []
            for k in range(2):
                nbr = ids_s[j, k, block]
                shard = nbr // ROWS
                col = (shard // 2) % NX
                rows.append(
                    ((shard // (2 * NX) * 2 + shard % 2) * 2 + col % 2) * ROWS + nbr % ROWS
                )
                bias.append(jnp.where(col // 2 == x1, 0.0, NEG))
            loaded.append((
                qq[slot, 0] if j == 0 else q_in[j, slot],
                jnp.concatenate([kv[0, rows[0]], kv[0, rows[1]]], axis=0),
                jnp.concatenate([kv[1, rows[0]], kv[1, rows[1]]], axis=0),
                jnp.where(lane < NBR, bias[0], bias[1]),
            ))
        scores = [
            lax.dot_general(q, keys, (((1,), (1,)), ((), ())), preferred_element_type=F32) + bias
            for q, keys, _, bias in loaded
        ]
        expo = [jnp.exp(s) for s in scores]
        denom = [jnp.sum(e, axis=-1, keepdims=True) for e in expo]
        down = [jnp.where(d > 1.0, 0.0625, 1.0) for d in denom]
        inverse = [jnp.where(d > 0.0, 1.0 / (d * w), 0.0) for d, w in zip(denom, down)]
        probs = [(e * w * v).astype(BF) for e, w, v in zip(expo, down, inverse)]
        parts = [
            jnp.dot(p, values, preferred_element_type=F32)
            for p, (_, _, values, _) in zip(probs, loaded)
        ]
        for n in range(0, len(items), 2):
            j = items[n][0]
            total = jnp.zeros((1, HD), F32)
            for a in range(2):
                r_out[j, pair, a * BLOCK : (a + 1) * BLOCK, :] = parts[n + a].astype(BF)
                total += jnp.sum(
                    jnp.where(offset == a * BLOCK, denom[n + a], 0.0), axis=0, keepdims=True
                )
            l_out[j, pair // 3, pl.ds(pair % 3, 1), :] = total

    def serve(pair, slots, parts):
        for g, first, count in parts:
            landed(q_in.at[pl.ds(1, 3), pl.ds(first, count)], q_rs.at[g])
        attend(pair, [(j, slot) for j in (1, 2, 3, 0) for slot in slots])
        for j in (2, 1, 3):
            send(r_out.at[j, pair], r_in.at[j, pair], 11, r_rs.at[pair], x_dev[j])

    ones = jnp.ones((16, HD), BF)

    def send_sums(third):
        for j in (2, 1, 3):
            send(l_out.at[j, third], l_in.at[j, third], 12, l_rs.at[third], x_dev[j])

    def column(row):
        hi = row.astype(BF).astype(F32)
        mid = (row - hi).astype(BF).astype(F32)
        lo = row - hi - mid
        terms = jnp.where(
            row_no == 0, hi, jnp.where(row_no == 1, mid, jnp.where(row_no == 2, lo, 0.0))
        )
        return lax.dot_general(
            terms.astype(BF), ones, (((0,), (0,)), ((), ())), preferred_element_type=F32
        )

    def merge(pair, slots):
        landed(r_in.at[pl.ds(1, 3), pair], r_rs.at[pair])
        todo = (
            (x0, (r_out, l_out, 0), (r_in, l_in, 2)),
            (1 - x0, (r_in, l_in, 1), (r_in, l_in, 3)),
        )
        weights, vals = [], []
        for _, *two in todo:
            la, lb = (sums[j, pair // 3, pl.ds(pair % 3, 1), :] for _, sums, j in two)
            weights.append(column(la / jnp.where(la + lb > 0.0, la + lb, 1.0)))
            vals.append([ref[j, pair].astype(F32) for ref, _, j in two])
        for (head, _, _), wa, (va, vb) in zip(todo, weights, vals):
            mixed = (wa * va + (1.0 - wa) * vb).astype(BF)
            columns = pl.ds(pl.multiple_of(head * HD, HD), HD)
            for a, slot in enumerate(slots):
                rows = pl.ds(pl.multiple_of(block_of(slot) * BLOCK, BLOCK), BLOCK)
                out[rows, columns] = mixed[a * BLOCK : (a + 1) * BLOCK]

    loads[0].wait()
    loads[1].wait()
    norm()
    pl.semaphore_wait(barrier, len(peers))
    w_far()
    z_first()
    loads[2].wait()
    for j in (1, 2, 3):
        send(ids_v.at[0], ids_v.at[j], 5, i_rs.at[0], x_dev[j])
    loads[3].wait()

    def keys(n, carry):
        part = bank_v.at[pl.ds(n * half, half)]
        pltpu.make_async_copy(part, part, lsem.at[4 + n]).wait()
        project(0, n)
        pass_on(0, n)
        return carry

    lax.fori_loop(0, 2, keys, 0)
    loads[6].wait()

    def values(n, carry):
        project(1, n)
        pass_on(1, n)
        return carry

    lax.fori_loop(0, 2, values, 0)
    loads[7].wait()
    queries(0)
    w_along_y()
    y_step(1, 0)
    neighbour(0)
    y_step(1, 1)
    neighbour(1)
    landed(ids_v.at[pl.ds(1, 3)], i_rs.at[0])
    to_smem = pltpu.make_async_copy(ids_v, ids_s, lsem.at[8])
    to_smem.start()
    z_step(1, 0)
    w_along_x()
    y_step(2, 0)
    z_step(1, 1)
    queries(1)
    y_step(1, 2)
    z_step(2, 0)
    y_step(2, 1)
    w_on()
    y_step(1, 3)
    w_last()
    z_step(2, 1)
    y_step(3, 0)
    queries(2)
    w_whole()
    far_queries(0)
    far_queries(1)
    y_step(2, 2)
    z_step(3, 0)
    y_step(3, 1)
    z_step(3, 1)
    y_step(2, 3)
    queries(3)
    far_queries(2)
    y_step(3, 2, ways=(1,))
    y_step(4, 0)
    y_step(3, 2, ways=(0,))
    y_step(3, 3, ways=(1,))
    relay(0)
    y_step(4, 1)
    y_step(4, 2)
    relay(1)
    y_step(3, 3, ways=(0,))
    y_step(4, 3)
    relay(2)
    to_smem.wait()
    landed(kv.at[0], b_rs.at[0])
    serve(0, (0, 5), [(0, 0, 1), (3, 5, 1)])

    def serve_near(n, carry):
        serve(1 + n, (1 + 2 * n, 2 + 2 * n), [(1 + n, 1 + 2 * n, 2)])
        return carry

    def serve_away(n, carry):
        first = HALF + 2 * n
        serve(3 + n, (first, first + 1), [(4 + n, first, 2)])
        return carry

    lax.fori_loop(0, 2, serve_near, 0)
    send_sums(0)
    lax.fori_loop(0, 3, serve_away, 0)
    send_sums(1)
    landed(l_in.at[pl.ds(1, 3), 0], l_rs.at[0])
    merge(0, (0, 5))

    def merge_near(n, carry):
        merge(1 + n, (1 + 2 * n, 2 + 2 * n))
        return carry

    def merge_away(n, carry):
        merge(3 + n, (HALF + 2 * n, HALF + 1 + 2 * n))
        return carry

    lax.fori_loop(0, 2, merge_near, 0)
    landed(l_in.at[pl.ds(1, 3), 1], l_rs.at[1])
    lax.fori_loop(0, 3, merge_away, 0)

    for family, like in enumerate((
        w2_v.at[pl.ds(0, 64)],
        w2_v.at[pl.ds(0, 7 * 64)],
        w2_v.at[pl.ds(0, 1536)],
        w2_v.at[pl.ds(0, D // 2)],
        zb.at[pl.ds(0, 5)],
        ids_v.at[pl.ds(1, 3)],
        kv.at[0, pl.ds(0, 112)],
        kv.at[0],
        kvs,
        q_in.at[pl.ds(1, 3)],
        q2,
        r_in.at[pl.ds(1, 3)],
        l_in.at[pl.ds(1, 3)],
    )):
        all_sent(like, family)


def per_device(hidden, norm_gain, query_weight, key_weight, value_weight, bank, neighbour_ids):
    hbm = pl.BlockSpec(memory_space=pl.ANY)
    dma = pltpu.SemaphoreType.DMA
    width = query_weight.shape[1]
    return pl.pallas_call(
        kernel,
        out_shape=pltpu.VMEM((NZ * BLOCK, width), BF),
        in_specs=[hbm] * 7,
        out_specs=pl.BlockSpec(memory_space=pltpu.VMEM),
        scratch_shapes=[
            pltpu.VMEM((BLOCK, D), BF),
            pltpu.VMEM((D, width), BF),
            pltpu.VMEM((D, width), BF),
            pltpu.VMEM((D, width), BF),
            pltpu.VMEM((D, width), BF),
            pltpu.VMEM((ROWS, NBR, D), BF),
            pltpu.VMEM((HALF, BLOCK, D), BF),
            pltpu.VMEM((2, NY * 2 * 2 * ROWS, NBR, HD), BF),
            pltpu.VMEM((2, ROWS, NBR, HD), BF),
            pltpu.VMEM((NZ, 2, BLOCK, HD), BF),
            pltpu.VMEM((HALF, 2, BLOCK, HD), BF),
            pltpu.VMEM((NX, NZ, BLOCK, HD), BF),
            pltpu.VMEM((NX, HALF, 2 * BLOCK, HD), BF),
            pltpu.VMEM((NX, HALF, 2 * BLOCK, HD), BF),
            pltpu.VMEM((NX, 2, NZ), jnp.int32),
            pltpu.SMEM((NX, 2, NZ), jnp.int32),
            dma((9,)),
            dma((13,)),
            dma((2, 3, 2)),
            dma((2, 4, 4)),
            dma((2,)),
            dma((1,)),
            dma((7,)),
            dma((6,)),
            dma((1,)),
            dma((1,)),
            dma((1,)),
            dma((2, 2)),
            dma((1,)),
            dma((3,)),
            pltpu.VMEM((1, D), F32),
            pltpu.VMEM((NX, 2, 8, HD), F32),
            pltpu.VMEM((NX, 2, 8, HD), F32),
            dma((2,)),
        ],
        compiler_params=pltpu.CompilerParams(
            collective_id=0, has_side_effects=True, vmem_limit_bytes=56 * 1024 * 1024
        ),
    )(
        hidden, norm_gain.reshape(1, D), query_weight, key_weight, value_weight, bank, neighbour_ids.T
    )


def solution(mesh):
    placed = (
        P(("db", "mp"), None),
        P(),
        P(None, "mp"),
        P(None, "mp"),
        P(None, "mp"),
        P("db", None, None),
        P("db", None),
    )
    return jax.shard_map(
        per_device, mesh=mesh, in_specs=placed, out_specs=P("db", "mp"), check_vma=False
    )
```

```python
import jax
import jax.numpy as jnp
from jax import lax
from jax.experimental import pallas as pl
from jax.experimental.pallas import tpu as pltpu
from jax.sharding import PartitionSpec as P

HD = 128
BLOCK = 64
NBR = 128
EPS = 1e-6
NX, NY, NZ = 4, 8, 12
D = 4096
ROWS = 4
NEG = -1e30
MESH = pl.DeviceIdType.MESH
BF = jnp.bfloat16
F32 = jnp.float32


GROUPS = ((0, 1), (1, 2), (3, 2), (5, 1), (6, 2), (8, 2), (10, 2))
HALF = NZ // 2


def kernel(
    hidden, gain, wq, wk, wv, bank, ids, out,
    hid_v, wq_v, w2_v, wk_v, wv_v, bank_v, zb, kv, kvs, qq, q2, q_in, r_out, r_in, ids_v, ids_s,
    lsem, s_sem, z_rs, y_rs, x_rs, b_rs, q_rs, r_rs, i_rs, w0_rs, wy_rs, wx_rs, wb_rs, f_rs,
    gain_v, l_out, l_in, l_rs,
):
    db = lax.axis_index("db")
    z = lax.axis_index("mp")
    c = db % 2
    x = (db // 2) % NX
    y = db // (2 * NX)
    x0 = x % 2
    x1 = x // 2
    turn = 1 - 2 * c

    def dev(yy, xx, cc, zz):
        return {"db": (yy * NX + xx) * 2 + cc, "mp": zz}

    xs = (x, x + 1 - 2 * x0, (x + 2) % NX, NX - 1 - x)
    z_dev = (dev(y, x, c, (z + NZ - turn) % NZ), dev(y, x, c, (z + NZ + turn) % NZ))
    far = dev(y, x, c, (z + HALF) % NZ)
    y_dev = (dev((y + 1) % NY, x, c, z), dev((y + NY - 1) % NY, x, c, z))
    y_others = tuple(dev((y + d) % NY, x, c, z) for d in (1, 7, 2, 6, 3, 5, 4))
    x_dev = tuple(dev(y, xx, c, z) for xx in xs)
    ring = (dev(y, (x + 1) % NX, c, z), dev(y, (x + NX - 1) % NX, c, z))
    sib = dev(y, x, 1 - c, z)
    peers = z_dev + (far,) + y_others + x_dev[1:] + (sib,)

    half = ROWS // 2
    loads = [
        pltpu.make_async_copy(a, b, lsem.at[n])
        for n, (a, b) in enumerate((
            (hidden, hid_v),
            (gain, gain_v),
            (ids, ids_v.at[0]),
            (wk, wk_v),
            (bank.at[pl.ds(0, half)], bank_v.at[pl.ds(0, half)]),
            (bank.at[pl.ds(half, half)], bank_v.at[pl.ds(half, half)]),
            (wv, wv_v),
            (wq, wq_v),
        ))
    ]
    for load in loads:
        load.start()
    barrier = pltpu.get_barrier_semaphore()
    for peer in peers:
        pl.semaphore_signal(barrier, inc=1, device_id=peer, device_id_type=MESH)

    def copy(src, dst, ss, rs, to):
        return pltpu.make_async_remote_copy(
            src_ref=src, dst_ref=dst, send_sem=ss, recv_sem=rs, device_id=to, device_id_type=MESH
        )

    def send(src, dst, family, rs, to):
        copy(src, dst, s_sem.at[family], rs, to).start()

    def landed(dst, rs):
        copy(dst, dst, s_sem.at[0], rs, sib).wait_recv()

    def all_sent(like, family):
        copy(like, like, s_sem.at[family], s_sem.at[family], sib).wait_send()

    def norm():
        def norm_rows(n, carry):
            rows = pl.ds(pl.multiple_of(n * 16, 16), 16)
            stream = hid_v[rows, :].astype(F32)
            factor = lax.rsqrt(jnp.mean(stream * stream, axis=-1, keepdims=True) + EPS)
            zb[0, rows, :] = (stream * factor * gain_v[...]).astype(BF)
            return carry

        lax.fori_loop(0, BLOCK // 16, norm_rows, 0)

    def w_rows(first, count):
        return w2_v.at[pl.ds(pl.multiple_of(first, 64), count)]

    def w_slice(yy):
        return w_rows(x * 1024 + c * 512 + yy * 64, 64)

    def w_far():
        first = pl.multiple_of(x * 1024 + c * 512 + y * 64, 64)
        send(wq.at[pl.ds(first, 64)], w_slice(y), 0, w0_rs.at[0], far)

    def w_along_y():
        landed(w_slice(y), w0_rs.at[0])
        for to in y_others:
            send(w_slice(y), w_slice(y), 1, wy_rs.at[0], to)

    def w_block(xx, cc):
        return w_rows(xx * 1024 + cc * 512, 512)

    def w_half(xx, cc, half):
        return w_rows(xx * 1024 + cc * 512 + half * 256, 256)

    def w_along_x():
        landed(w2_v.at[pl.ds(0, 7 * 64)], wy_rs.at[0])
        own_block = w_block(x, c)
        for way in range(2):
            send(own_block, own_block, 2, wx_rs.at[way, 0], ring[way])
        send(own_block, own_block, 3, wb_rs.at[0], sib)

    def w_from(way):
        return (x + NX - 1) % NX if way == 0 else (x + 1) % NX

    def w_on():
        for way in range(2):
            block = w_block(w_from(way), c)
            landed(block, wx_rs.at[way, 0])
            half = w_half(w_from(way), c, way)
            send(half, half, 2, wx_rs.at[way, 1], ring[way])
            send(block, block, 3, wb_rs.at[0], sib)

    def w_last():
        for way in range(2):
            half = w_half((x + 2) % NX, c, way)
            landed(half, wx_rs.at[way, 1])
            send(half, half, 3, wb_rs.at[0], sib)

    def w_whole():
        landed(w2_v.at[pl.ds(0, D // 2)], wb_rs.at[0])

    STEPS = (3, 2)

    def z_part(slot, sub):
        return zb.at[slot, pl.ds(sub * 32, 32), :]

    def z_slot(way, s):
        return 0 if s == 0 else 2 * s - 1 + way

    def z_send(way, s, sub):
        send(
            z_part(z_slot(way, s), sub), z_part(z_slot(way, s + 1), sub),
            4, z_rs.at[way, s, sub], z_dev[way],
        )

    def z_step(s, sub):
        for way in range(2):
            if s <= STEPS[way]:
                landed(z_part(z_slot(way, s), sub), z_rs.at[way, s - 1, sub])
                if s < STEPS[way]:
                    z_send(way, s, sub)

    def z_first():
        for sub in range(2):
            for way in range(2):
                z_send(way, 0, sub)

    def unit(yy, cc, bit):
        return ((yy * 2 + cc) * 2 + bit) * ROWS

    own = unit(y, c, x0)

    def project(which, n):
        got = jnp.dot(
            bank_v[pl.ds(n * half, half)].reshape(half * NBR, D), (wk_v, wv_v)[which][...],
            preferred_element_type=F32,
        )
        low, high = got[:, :HD], got[:, HD:]
        mine = jnp.where(x0 == 0, low, high).astype(BF)
        other = jnp.where(x0 == 0, high, low).astype(BF)
        for a in range(half):
            kv[which, own + n * half + a] = mine[a * NBR : (a + 1) * NBR]
            kvs[which, n * half + a] = other[a * NBR : (a + 1) * NBR]

    def pass_on(which, n):
        part = kv.at[which, pl.ds(own + n * half, half)]
        for way in range(2):
            send(part, part, 6, y_rs.at[way, 0, which], y_dev[way])
        send(kvs.at[which, pl.ds(n * half, half)], part, 8, x_rs.at[which], x_dev[1])
        send(part, part, 7, b_rs.at[0], sib)

    def y_at(way, s):
        return (y + NY - s) % NY if way == 0 else (y + s) % NY

    def kv_part(yy, cc, sub):
        return kv.at[sub % 2, pl.ds(unit(yy, cc, x0 if sub < 2 else 1 - x0), ROWS)]

    def y_send(way, s, sub):
        part = kv_part(y_at(way, s), c, sub)
        send(part, part, 6, y_rs.at[way, s, sub], y_dev[way])

    def b_send(way, s, sub):
        part = kv_part(y_at(way, s), c, sub)
        send(part, part, 7, b_rs.at[0], sib)

    def y_needed(way, s, sub):
        return s < 4 or sub // 2 == way

    def y_first(sub):
        for way in range(2):
            y_send(way, 0, sub)
        b_send(0, 0, sub)

    def y_step(s, *subs, ways=(0, 1)):
        for sub in subs:
            for way in ways:
                if y_needed(way, s, sub):
                    part = kv_part(y_at(way, s), c, sub)
                    landed(part, y_rs.at[way, s - 1, sub])
                    if s < 4 and y_needed(way, s + 1, sub):
                        y_send(way, s, sub)
                    b_send(way, s, sub)

    def neighbour(which):
        landed(kv_part(y, c, 2 + which), x_rs.at[which])
        y_first(2 + which)

    scale = HD ** (-0.5)

    def store_queries(got, ref, first, count):
        got = got * scale
        low, high = got[:, :HD], got[:, HD:]
        mine = jnp.where(x0 == 0, low, high).astype(BF)
        other = jnp.where(x0 == 0, high, low).astype(BF)
        for a in range(count):
            ref[first + a, 0] = mine[a * BLOCK : (a + 1) * BLOCK]
            ref[first + a, 1] = other[a * BLOCK : (a + 1) * BLOCK]

    def rows_of_slots(first, count):
        return zb[first : first + count].reshape(count * BLOCK, D)

    def q_along_x(g):
        first, count = GROUPS[g]
        for j in (2, 1, 3):
            send(
                qq.at[pl.ds(first, count), 0 if j == 2 else 1], q_in.at[j, pl.ds(first, count)],
                9, q_rs.at[g], x_dev[j],
            )

    def queries(g):
        first, count = GROUPS[g]
        got = jnp.dot(rows_of_slots(first, count), wq_v[...], preferred_element_type=F32)
        store_queries(got, qq, first, count)
        q_along_x(g)

    def far_queries(n):
        got = jnp.dot(rows_of_slots(2 * n, 2), w2_v[...], preferred_element_type=F32)
        store_queries(got, q2, 2 * n, 2)
        send(
            q2.at[pl.ds(2 * n, 2)], qq.at[pl.ds(HALF + 2 * n, 2)], 10, f_rs.at[n], far
        )

    def relay(n):
        landed(qq.at[pl.ds(HALF + 2 * n, 2)], f_rs.at[n])
        q_along_x(4 + n)

    def block_of(slot):
        u = slot % HALF
        sign = turn * (2 * (u % 2) - 1)
        return (z + NZ + HALF * (slot // HALF) + sign * ((u + 1) // 2)) % NZ

    offset = lax.broadcasted_iota(jnp.int32, (BLOCK, HD), 1) - lax.broadcasted_iota(
        jnp.int32, (BLOCK, HD), 0
    )
    row_no = lax.broadcasted_iota(jnp.int32, (16, HD), 0)

    lane = lax.broadcasted_iota(jnp.int32, (1, 2 * NBR), 1)

    def attend(pair, items):
        loaded = []
        for j, slot in items:
            block = block_of(slot)
            rows, bias = [], []
            for k in range(2):
                nbr = ids_s[j, k, block]
                shard = nbr // ROWS
                col = (shard // 2) % NX
                rows.append(
                    ((shard // (2 * NX) * 2 + shard % 2) * 2 + col % 2) * ROWS + nbr % ROWS
                )
                bias.append(jnp.where(col // 2 == x1, 0.0, NEG))
            loaded.append((
                qq[slot, 0] if j == 0 else q_in[j, slot],
                jnp.concatenate([kv[0, rows[0]], kv[0, rows[1]]], axis=0),
                jnp.concatenate([kv[1, rows[0]], kv[1, rows[1]]], axis=0),
                jnp.where(lane < NBR, bias[0], bias[1]),
            ))
        scores = [
            lax.dot_general(q, keys, (((1,), (1,)), ((), ())), preferred_element_type=F32) + bias
            for q, keys, _, bias in loaded
        ]
        expo = [jnp.exp(s) for s in scores]
        denom = [jnp.sum(e, axis=-1, keepdims=True) for e in expo]
        down = [jnp.where(d > 1.0, 0.0625, 1.0) for d in denom]
        inverse = [jnp.where(d > 0.0, 1.0 / (d * w), 0.0) for d, w in zip(denom, down)]
        probs = [(e * w * v).astype(BF) for e, w, v in zip(expo, down, inverse)]
        parts = [
            jnp.dot(p, values, preferred_element_type=F32)
            for p, (_, _, values, _) in zip(probs, loaded)
        ]
        for n in range(0, len(items), 2):
            j = items[n][0]
            total = jnp.zeros((1, HD), F32)
            for a in range(2):
                r_out[j, pair, a * BLOCK : (a + 1) * BLOCK, :] = parts[n + a].astype(BF)
                total += jnp.sum(
                    jnp.where(offset == a * BLOCK, denom[n + a], 0.0), axis=0, keepdims=True
                )
            l_out[j, pair // 3, pl.ds(pair % 3, 1), :] = total

    def serve(pair, slots, parts):
        for g, first, count in parts:
            landed(q_in.at[pl.ds(1, 3), pl.ds(first, count)], q_rs.at[g])
        attend(pair, [(j, slot) for j in (1, 2, 3, 0) for slot in slots])
        for j in (2, 1, 3):
            send(r_out.at[j, pair], r_in.at[j, pair], 11, r_rs.at[pair], x_dev[j])

    ones = jnp.ones((16, HD), BF)

    def send_sums(third):
        for j in (2, 1, 3):
            send(l_out.at[j, third], l_in.at[j, third], 12, l_rs.at[third], x_dev[j])

    def column(row):
        hi = row.astype(BF).astype(F32)
        mid = (row - hi).astype(BF).astype(F32)
        lo = row - hi - mid
        terms = jnp.where(
            row_no == 0, hi, jnp.where(row_no == 1, mid, jnp.where(row_no == 2, lo, 0.0))
        )
        return lax.dot_general(
            terms.astype(BF), ones, (((0,), (0,)), ((), ())), preferred_element_type=F32
        )

    def merge(pair, slots):
        landed(r_in.at[pl.ds(1, 3), pair], r_rs.at[pair])
        todo = (
            (x0, (r_out, l_out, 0), (r_in, l_in, 2)),
            (1 - x0, (r_in, l_in, 1), (r_in, l_in, 3)),
        )
        weights, vals = [], []
        for _, *two in todo:
            la, lb = (sums[j, pair // 3, pl.ds(pair % 3, 1), :] for _, sums, j in two)
            weights.append(column(la / jnp.where(la + lb > 0.0, la + lb, 1.0)))
            vals.append([ref[j, pair].astype(F32) for ref, _, j in two])
        for (head, _, _), wa, (va, vb) in zip(todo, weights, vals):
            mixed = (wa * va + (1.0 - wa) * vb).astype(BF)
            columns = pl.ds(pl.multiple_of(head * HD, HD), HD)
            for a, slot in enumerate(slots):
                rows = pl.ds(pl.multiple_of(block_of(slot) * BLOCK, BLOCK), BLOCK)
                out[rows, columns] = mixed[a * BLOCK : (a + 1) * BLOCK]

    pl.semaphore_wait(barrier, len(peers))
    w_far()
    loads[0].wait()
    loads[1].wait()
    norm()
    z_first()
    loads[2].wait()
    for j in (1, 2, 3):
        send(ids_v.at[0], ids_v.at[j], 5, i_rs.at[0], x_dev[j])
    loads[3].wait()

    def keys(n, carry):
        part = bank_v.at[pl.ds(n * half, half)]
        pltpu.make_async_copy(part, part, lsem.at[4 + n]).wait()
        project(0, n)
        pass_on(0, n)
        return carry

    lax.fori_loop(0, 2, keys, 0)
    loads[6].wait()

    def values(n, carry):
        project(1, n)
        pass_on(1, n)
        return carry

    lax.fori_loop(0, 2, values, 0)
    loads[7].wait()
    queries(0)
    w_along_y()
    y_step(1, 0)
    neighbour(0)
    y_step(1, 1)
    neighbour(1)
    landed(ids_v.at[pl.ds(1, 3)], i_rs.at[0])
    to_smem = pltpu.make_async_copy(ids_v, ids_s, lsem.at[8])
    to_smem.start()
    z_step(1, 0)
    w_along_x()
    y_step(2, 0)
    z_step(1, 1)
    queries(1)
    y_step(1, 2)
    z_step(2, 0)
    y_step(2, 1)
    w_on()
    y_step(1, 3)
    w_last()
    z_step(2, 1)
    y_step(3, 0)
    queries(2)
    w_whole()
    far_queries(0)
    far_queries(1)
    y_step(2, 2)
    z_step(3, 0)
    y_step(3, 1)
    z_step(3, 1)
    y_step(2, 3)
    queries(3)
    far_queries(2)
    y_step(3, 2, ways=(1,))
    y_step(4, 0)
    y_step(3, 2, ways=(0,))
    y_step(3, 3, ways=(1,))
    relay(0)
    y_step(4, 1)
    y_step(4, 2)
    relay(1)
    y_step(3, 3, ways=(0,))
    y_step(4, 3)
    relay(2)
    to_smem.wait()
    landed(kv.at[0], b_rs.at[0])
    serve(0, (0, 5), [(0, 0, 1), (3, 5, 1)])

    def serve_near(n, carry):
        serve(1 + n, (1 + 2 * n, 2 + 2 * n), [(1 + n, 1 + 2 * n, 2)])
        return carry

    def serve_away(n, carry):
        first = HALF + 2 * n
        serve(3 + n, (first, first + 1), [(4 + n, first, 2)])
        return carry

    lax.fori_loop(0, 2, serve_near, 0)
    send_sums(0)
    lax.fori_loop(0, 3, serve_away, 0)
    send_sums(1)
    landed(l_in.at[pl.ds(1, 3), 0], l_rs.at[0])
    merge(0, (0, 5))

    def merge_near(n, carry):
        merge(1 + n, (1 + 2 * n, 2 + 2 * n))
        return carry

    def merge_away(n, carry):
        merge(3 + n, (HALF + 2 * n, HALF + 1 + 2 * n))
        return carry

    lax.fori_loop(0, 2, merge_near, 0)
    landed(l_in.at[pl.ds(1, 3), 1], l_rs.at[1])
    lax.fori_loop(0, 3, merge_away, 0)

    for family, like in enumerate((
        w2_v.at[pl.ds(0, 64)],
        w2_v.at[pl.ds(0, 7 * 64)],
        w2_v.at[pl.ds(0, 1536)],
        w2_v.at[pl.ds(0, D // 2)],
        zb.at[pl.ds(0, 5)],
        ids_v.at[pl.ds(1, 3)],
        kv.at[0, pl.ds(0, 112)],
        kv.at[0],
        kvs,
        q_in.at[pl.ds(1, 3)],
        q2,
        r_in.at[pl.ds(1, 3)],
        l_in.at[pl.ds(1, 3)],
    )):
        all_sent(like, family)


def per_device(hidden, norm_gain, query_weight, key_weight, value_weight, bank, neighbour_ids):
    hbm = pl.BlockSpec(memory_space=pl.ANY)
    dma = pltpu.SemaphoreType.DMA
    width = query_weight.shape[1]
    return pl.pallas_call(
        kernel,
        out_shape=pltpu.VMEM((NZ * BLOCK, width), BF),
        in_specs=[hbm] * 7,
        out_specs=pl.BlockSpec(memory_space=pltpu.VMEM),
        scratch_shapes=[
            pltpu.VMEM((BLOCK, D), BF),
            pltpu.VMEM((D, width), BF),
            pltpu.VMEM((D, width), BF),
            pltpu.VMEM((D, width), BF),
            pltpu.VMEM((D, width), BF),
            pltpu.VMEM((ROWS, NBR, D), BF),
            pltpu.VMEM((HALF, BLOCK, D), BF),
            pltpu.VMEM((2, NY * 2 * 2 * ROWS, NBR, HD), BF),
            pltpu.VMEM((2, ROWS, NBR, HD), BF),
            pltpu.VMEM((NZ, 2, BLOCK, HD), BF),
            pltpu.VMEM((HALF, 2, BLOCK, HD), BF),
            pltpu.VMEM((NX, NZ, BLOCK, HD), BF),
            pltpu.VMEM((NX, HALF, 2 * BLOCK, HD), BF),
            pltpu.VMEM((NX, HALF, 2 * BLOCK, HD), BF),
            pltpu.VMEM((NX, 2, NZ), jnp.int32),
            pltpu.SMEM((NX, 2, NZ), jnp.int32),
            dma((9,)),
            dma((13,)),
            dma((2, 3, 2)),
            dma((2, 4, 4)),
            dma((2,)),
            dma((1,)),
            dma((7,)),
            dma((6,)),
            dma((1,)),
            dma((1,)),
            dma((1,)),
            dma((2, 2)),
            dma((1,)),
            dma((3,)),
            pltpu.VMEM((1, D), F32),
            pltpu.VMEM((NX, 2, 8, HD), F32),
            pltpu.VMEM((NX, 2, 8, HD), F32),
            dma((2,)),
        ],
        compiler_params=pltpu.CompilerParams(
            collective_id=0, has_side_effects=True, vmem_limit_bytes=56 * 1024 * 1024
        ),
    )(
        hidden, norm_gain.reshape(1, D), query_weight, key_weight, value_weight, bank, neighbour_ids.T
    )


def solution(mesh):
    placed = (
        P(("db", "mp"), None),
        P(),
        P(None, "mp"),
        P(None, "mp"),
        P(None, "mp"),
        P("db", None, None),
        P("db", None),
    )
    return jax.shard_map(
        per_device, mesh=mesh, in_specs=placed, out_specs=P("db", "mp"), check_vma=False
    )
```
